128 devices in a mesh: row: 16 (over z_hi, y, core), col: 8 (over x, z_lo).
Axes of the slice: x: 4, y: 4, z: 4 (z_hi: 2, z_lo: 2; z = z_hi * 2 + z_lo), core: 2. Of those that a mesh axis runs over, the one named last changes fastest.
Arguments:
- traces: bfloat16 [65536, 8192], P(('row', 'col')), may hold values from -60 to 60
- seg_owner: int32 [65536, 1], P(('row', 'col')), may hold values from 0 to 127; in each aligned block of 512 rows (0 to 511, 512 to 1023, ...) at most 16 rows name the same one
- seg_slot: int32 [65536], P(('row', 'col')), may hold values from 0 to 767
- white_width: int32 [1024], replicated, may hold values from 1 to 8
- band_bins: int32 [256], replicated, may hold values from 513 to 1023, as said below
Outputs:
- cross_spectra: bfloat16 [1024, 1024, 512], P('row', 'col')
The draws below stay inside these ranges and needn't reach their ends.
Inputs may be any that keep to these rules, and one draw needn't show every extreme that they name: `seg_owner`: among the 512 segments held by one device, no owner is named more than 16 times, a bound that some block reaches. `band_bins`: strictly increasing.
All inputs are finite; a program needn't handle non-finite values.
Results may differ from the reference program's by a relative error of at most 0.008.
Values may be sent and summed in bfloat16 or wider, within the bound.
No kernel may reach another device: no remote copies, remote signals or barrier semaphores. Data moves between devices by JAX's collectives and lax.ppermute only.
A program may use at most 192 MiB of HBM per device.

```python
import math
import jax
import jax.numpy as jnp
import numpy as np
from jax import lax

L = 8192
NBAND = 256
HALF = 64
WMAX = 8
ST_DEV = 8
HOURS = 96
SEG_DEV = 512
STATIONS = 1024
SEGMENTS = 65536
CAP = 16
N_ROW = 16
N_COL = 8
DEVICES = 128


def draw_traces(key, part):
    key = jax.random.fold_in(key, 11)
    noise_key, level_key = jax.random.split(key)
    pieces = 32
    levels = jax.random.uniform(level_key, (SEGMENTS, pieces), dtype=jnp.float32)
    noise = jnp.clip(jax.random.normal(noise_key, (SEGMENTS, L), dtype=jnp.float32), -4.0, 4.0)
    envelope = 10.0 ** levels
    envelope = jnp.repeat(envelope, L // pieces, axis=1)
    return (noise * envelope).astype(jnp.bfloat16)


def draw_band_bins(key, part):
    key = jax.random.fold_in(key, 23)
    highest = L // 16 - 1 + 2 * NBAND
    gaps = jax.random.randint(key, (NBAND - 1,), 1, 3)
    offsets = jnp.cumsum(gaps[::-1])[::-1]
    offsets = jnp.concatenate([offsets, jnp.zeros((1,), jnp.int32)])
    return (highest - offsets).astype(jnp.int32)


def touch_ends(values, own_key, least, high):
    shape = values.shape
    index_at = [jax.random.randint(jax.random.fold_in(own_key, axis), (), 0, shape[axis]) for axis in range(len(shape))]
    values = values.at[tuple(index_at)].set(least)
    longest = shape.index(max(shape))
    index_at[longest] = (index_at[longest] + 1) % shape[longest]
    return values.at[tuple(index_at)].set(high)


def assign_block(rng, own, number, rows, count, top, limit, slope):
    ranking = jax.random.permutation(rng, count)
    heavy_load, ordinary = shares(count, rows * top, limit, slope, True), shares(count, rows * top, limit, slope, False)
    places = jnp.arange(count)

    def named(tallies, turn):
        used = int((tallies > 0).sum())
        fixed = max(1, used // 4)
        passed = fixed + (places - fixed + turn * (used - fixed)) % max(1, count - fixed)
        return jnp.zeros((count,), jnp.int32).at[ranking[jnp.where(places < fixed, places, passed)]].set(jnp.asarray(tallies, jnp.int32))

    tallies = jnp.where(number % 4 == 0, named(heavy_load, number // 4), named(ordinary, number - number // 4 - 1))
    mixed = jax.random.permutation(jax.random.fold_in(own, 3), count)
    donor, sink = mixed[0:count // 2 * 2:2], mixed[1:count // 2 * 2:2]
    margin = jnp.minimum(tallies[donor] - 1, limit - tallies[sink]) // 2
    margin = jnp.where((donor == ranking[0]) | (sink == ranking[0]) | (tallies[sink] == 0), 0, jnp.maximum(margin, 0))
    passed = jax.random.randint(jax.random.fold_in(own, 4), (count // 2,), 0, 1 << 20) % (margin + 1)
    tallies = tallies.at[donor].add(-passed).at[sink].add(passed)
    items = jnp.searchsorted(jnp.cumsum(tallies), jnp.arange(rows * top), side="right").astype(jnp.int32)
    table = items.reshape(top, rows).T
    table = table[jax.random.permutation(jax.random.fold_in(own, 1), rows)]
    turn = jax.random.randint(jax.random.fold_in(own, 2), (rows, 1), 0, top)
    return jnp.take_along_axis(table, (jnp.arange(top)[None, :] + turn) % top, axis=1)


def shares(number_of, total, limit, lean, full):
    weights = [(1 << 20) // math.isqrt(rank ** lean) + 1 for rank in range(1, number_of + 1)]
    largest = limit if full else min(limit, max(-(-total // number_of), total * weights[0] // sum(weights)))
    least = 1 if total - largest >= number_of - 1 else 0
    given, spare = [largest] + [least] * (number_of - 1), total - largest - least * (number_of - 1)
    while spare > 0:
        free = [i for i in range(1, number_of) if given[i] < largest] or [i for i in range(1, number_of) if given[i] < limit]
        mass, left = sum([weights[i] for i in free]), spare
        for i in free:
            addition = min(limit - given[i], max(1, left * weights[i] // mass), spare)
            given[i] = given[i] + addition
            spare = spare - addition
    return np.array(given)


def setup_inputs(seed: int = 0) -> dict:
    keys = jax.random.split(jax.random.key(seed), 6)
    traces = draw_traces(jax.random.fold_in(keys[5], 71), 0)
    seg_owner_keys = jax.random.split(jax.random.fold_in(keys[1], 1), SEGMENTS // SEG_DEV)
    seg_owner_turns = jax.random.permutation(jax.random.fold_in(keys[1], 3), SEGMENTS // SEG_DEV)
    seg_owner = jax.vmap(lambda own, number: assign_block(jax.random.fold_in(keys[1], 2), own, number, SEG_DEV, DEVICES, 1, CAP, 2))(seg_owner_keys, seg_owner_turns).reshape((SEGMENTS, 1))
    seg_slot = touch_ends(jax.random.randint(keys[2], (SEGMENTS,), 0, ST_DEV * HOURS), jax.random.fold_in(keys[2], 1), 0, (ST_DEV * HOURS) - 1).astype(jnp.int32)
    white_width = touch_ends(jax.random.randint(keys[3], (STATIONS,), 1, WMAX + 1), jax.random.fold_in(keys[3], 1), 1, WMAX).astype(jnp.int32)
    band_bins = draw_band_bins(jax.random.fold_in(keys[5], 71), 0)
    return {"traces": traces, "seg_owner": seg_owner, "seg_slot": seg_slot, "white_width": white_width, "band_bins": band_bins}


EPS = 1e-05
FLOOR = 0.5

def dft_table(band_bins, length):
    times = lax.broadcasted_iota(jnp.int32, (length, band_bins.shape[0]), 0)
    phase = times * band_bins[None, :].astype(jnp.int32) % length
    angle = phase.astype(jnp.float32) * (2.0 * math.pi / length)
    return jnp.concatenate([jnp.cos(angle), -jnp.sin(angle)], axis=1).astype(jnp.bfloat16)

def normalize(segments, half):
    values = segments.astype(jnp.float32)
    length = values.shape[1]
    running = jnp.cumsum(jnp.abs(values), axis=1)
    running = jnp.concatenate([jnp.zeros((values.shape[0], 1), jnp.float32), running], axis=1)
    upper = jnp.pad(running[:, half + 1:], ((0, 0), (0, half)), mode='edge')
    lower = jnp.pad(running[:, :length - half], ((0, 0), (half, 0)))
    places = lax.broadcasted_iota(jnp.int32, (1, length), 1)
    counts = jnp.minimum(places + half, length - 1) - jnp.maximum(places - half, 0) + 1
    means = (upper - lower) / counts.astype(jnp.float32)
    return (values / (means + EPS)).astype(jnp.bfloat16)

def whiten(spectrum, widths, wmax):
    nband = spectrum.shape[1] // 2
    real_part = spectrum[:, :nband]
    imag_part = spectrum[:, nband:]
    amplitude = jnp.sqrt(real_part * real_part + imag_part * imag_part)
    padded_amp = jnp.pad(amplitude, ((0, 0), (wmax, wmax)))
    padded_one = jnp.pad(jnp.ones_like(amplitude), ((0, 0), (wmax, wmax)))
    total = amplitude
    number = jnp.ones_like(amplitude)
    chosen = jnp.zeros_like(amplitude)
    for width in range(1, wmax + 1):
        total = total + padded_amp[:, wmax - width:wmax - width + nband] + padded_amp[:, wmax + width:wmax + width + nband]
        number = number + padded_one[:, wmax - width:wmax - width + nband] + padded_one[:, wmax + width:wmax + width + nband]
        chosen = jnp.where(widths[:, None] == width, total / number, chosen)
    factor = 1.0 / jnp.maximum(chosen, FLOOR)
    return (spectrum * jnp.concatenate([factor, factor], axis=1)).astype(jnp.bfloat16)

def lookup(stations, table_values):
    hits = stations[:, None] == lax.broadcasted_iota(jnp.int32, (1, table_values.shape[0]), 1)
    return lax.optimization_barrier(jnp.sum(jnp.where(hits, table_values[None, :], 0), axis=1)).astype(jnp.int32)

def transform(segments, widths, table):
    normalized = normalize(segments, HALF)
    spectrum = jnp.dot(normalized, table, preferred_element_type=jnp.float32) * (1.0 / math.sqrt(L))
    return whiten(spectrum, widths, WMAX)

def cross_block(row_spec, col_spec):
    left = row_spec.astype(jnp.float32)
    right = col_spec.astype(jnp.float32)
    left_real = jnp.concatenate([left[..., :NBAND], left[..., NBAND:]], axis=1)
    left_imag = jnp.concatenate([left[..., NBAND:], -left[..., :NBAND]], axis=1)
    right_both = jnp.concatenate([right[..., :NBAND], right[..., NBAND:]], axis=1)
    real_out = jnp.einsum('akf,bkf->abf', left_real, right_both, precision=lax.Precision.HIGHEST)
    imag_out = jnp.einsum('akf,bkf->abf', left_imag, right_both, precision=lax.Precision.HIGHEST)
    return jnp.concatenate([real_out, imag_out], axis=2).astype(jnp.bfloat16)

def reference(traces, seg_owner, seg_slot, white_width, band_bins):
    devices = N_ROW * N_COL
    table = dft_table(band_bins, L)
    owners = seg_owner[:, 0].astype(jnp.int32)
    stations = owners * ST_DEV + seg_slot // HOURS
    widths = lookup(stations, white_width)
    groups = traces.reshape(devices, SEG_DEV, L)
    width_groups = widths.reshape(devices, SEG_DEV)
    whitened = lax.map(lambda pair: transform(pair[0], pair[1], table), (groups, width_groups))
    whitened = whitened.reshape(devices * SEG_DEV, 2 * NBAND)
    global_slot = owners * (ST_DEV * HOURS) + seg_slot
    summed = jax.ops.segment_sum(whitened.astype(jnp.float32), global_slot, num_segments=STATIONS * HOURS)
    station_spec = summed.astype(jnp.bfloat16).reshape(STATIONS, HOURS, 2 * NBAND)
    arranged = station_spec.reshape(N_ROW, N_COL, ST_DEV, HOURS, 2 * NBAND)
    columns = jnp.transpose(arranged, (1, 0, 2, 3, 4)).reshape(STATIONS, HOURS, 2 * NBAND)
    row_blocks = station_spec.reshape(N_ROW, N_COL * ST_DEV, HOURS, 2 * NBAND)
    result = lax.map(lambda block: cross_block(block, columns), row_blocks)
    return result.reshape(STATIONS, STATIONS, 2 * NBAND)
```

```python
import functools
import math

import jax
import jax.numpy as jnp
from jax import lax
from jax.experimental import pallas as pl
from jax.experimental.pallas import tpu as pltpu
from jax.sharding import Mesh, PartitionSpec as P

L = 8192
NBAND = 256
HALF = 64
WMAX = 8
ST_DEV = 8
HOURS = 96
CAP = 16
EPS = 1e-05
FLOOR = 0.5

AXES = ("zh", "y", "core", "x", "zl")
DEVICES = 128
SEGS = 512
STEP = 1024
STEPS = L // STEP
ROWS = 80
PAIRS = 64
WIDE = 4 * HOURS
F32 = jnp.float32
BF16 = jnp.bfloat16


def iota(shape, axis):
    return lax.broadcasted_iota(jnp.int32, shape, axis)


def transform_kernel(
    main, before, after, owner_col, owner_row, slot_col, width_row, bins,
    send, low_cos, low_sin, high_cos, high_sin, band, magnitude, normal, table, total,
):
    step = pl.program_id(0)

    @pl.when(step == 0)
    def _():
        unit = 2.0 * math.pi / L
        phase = (iota((128, NBAND), 0) * bins[...]) & (L - 1)
        angle = phase.astype(F32) * unit
        low_cos[...] = jnp.cos(angle)
        low_sin[...] = jnp.sin(angle)
        phase = (iota((64, NBAND), 0) * 128 * bins[...]) & (L - 1)
        angle = phase.astype(F32) * unit
        high_cos[...] = jnp.cos(angle)
        high_sin[...] = jnp.sin(angle)
        offset = iota((512, 256), 0) - 128 - iota((512, 256), 1)
        band[...] = jnp.where(jnp.abs(offset) <= HALF, 1.0, 0.0).astype(BF16)
        total[...] = jnp.zeros_like(total)

    for part in range(STEP // 128):
        high = step * (STEP // 128) + part
        cos_high = high_cos[pl.ds(high, 1), :]
        sin_high = high_sin[pl.ds(high, 1), :]
        rows = slice(part * 128, part * 128 + 128)
        table[rows, :NBAND] = (cos_high * low_cos[...] - sin_high * low_sin[...]).astype(BF16)
        table[rows, NBAND:] = (-(sin_high * low_cos[...] + cos_high * low_sin[...])).astype(BF16)

    magnitude[:, 128 : 128 + STEP] = jnp.abs(main[...])
    magnitude[:, :128] = jnp.where(step > 0, jnp.abs(before[...]), jnp.zeros((), BF16))
    magnitude[:, 128 + STEP :] = jnp.where(
        step < STEPS - 1, jnp.abs(after[...]), jnp.zeros((), BF16)
    )
    for part in range(STEP // 256):
        sums = jnp.dot(
            magnitude[:, part * 256 : part * 256 + 512], band[...], preferred_element_type=F32
        )
        place = step * STEP + part * 256 + iota((1, 256), 1)
        count = jnp.minimum(place + HALF, L - 1) - jnp.maximum(place - HALF, 0) + 1
        count = count.astype(F32)
        below = sums + count * EPS
        inverse = pl.reciprocal(below, approx=True)
        inverse = inverse * (2.0 - below * inverse)
        values = main[:, part * 256 : part * 256 + 256].astype(F32)
        normal[:, part * 256 : part * 256 + 256] = (values * (count * inverse)).astype(BF16)
    total[...] += jnp.dot(normal[...], table[...], preferred_element_type=F32)

    @pl.when(step == STEPS - 1)
    def _():
        slots = slot_col[...]
        station = jnp.zeros_like(slots)
        for edge in range(1, ST_DEV):
            station += (slots >= edge * HOURS).astype(jnp.int32)
        hour = slots - station * HOURS
        whole = owner_col[...] * ST_DEV + station
        hits = whole == iota((1, DEVICES * ST_DEV), 1)
        widths = jnp.sum(jnp.where(hits, width_row[...], 0).astype(F32), axis=1, keepdims=True)
        widths = widths.astype(jnp.int32)
        real = total[:, :NBAND] * (1.0 / math.sqrt(L))
        imag = total[:, NBAND:] * (1.0 / math.sqrt(L))
        amplitude = jnp.sqrt(real * real + imag * imag)
        lane = iota((1, NBAND), 1)
        smooth = amplitude
        for width in range(1, WMAX + 1):
            up = pltpu.roll(amplitude, width, 1)
            down = pltpu.roll(amplitude, NBAND - width, 1)
            both = jnp.where(lane >= width, up, 0.0) + jnp.where(lane < NBAND - width, down, 0.0)
            smooth += jnp.where(widths >= width, both, 0.0)
        number = jnp.minimum(lane + widths, NBAND - 1) - jnp.maximum(lane - widths, 0) + 1
        factor = 1.0 / jnp.maximum(smooth / number.astype(F32), FLOOR)
        lanes = iota((SEGS, 128), 1)
        extra = jnp.where(
            lanes == 0, station, jnp.where(lanes == 1, hour, jnp.where(lanes == 2, 1, 0))
        )
        whitened = jnp.concatenate(
            [
                (real * factor).astype(BF16),
                (imag * factor).astype(BF16),
                extra.astype(F32).astype(BF16),
            ],
            axis=1,
        )
        same = (owner_col[...] == owner_row[...]) & (iota((SEGS, SEGS), 0) < iota((SEGS, SEGS), 1))
        rank = jnp.sum(same.astype(F32), axis=0, keepdims=True).astype(jnp.int32)
        target = owner_row[...] * CAP + rank
        for part in range(4):
            chosen = target == iota((512, SEGS), 0) + part * 512
            chosen = jnp.where(chosen, 1.0, 0.0).astype(BF16)
            picked = jnp.dot(chosen, whitened, preferred_element_type=F32).astype(BF16)
            for tile in range(5):
                send[part * 32 : part * 32 + 32, tile * CAP : tile * CAP + CAP, :] = picked[
                    :, tile * 128 : tile * 128 + 128
                ].reshape(32, CAP, 128)


def transform(traces, seg_owner, seg_slot, white_width, band_bins):
    return pl.pallas_call(
        transform_kernel,
        grid=(STEPS,),
        in_specs=[
            pl.BlockSpec((SEGS, STEP), lambda k: (0, k)),
            pl.BlockSpec((SEGS, 128), lambda k: (0, jnp.maximum(k * (STEP // 128) - 1, 0))),
            pl.BlockSpec(
                (SEGS, 128), lambda k: (0, jnp.minimum((k + 1) * (STEP // 128), L // 128 - 1))
            ),
            pl.BlockSpec((SEGS, 1), lambda k: (0, 0)),
            pl.BlockSpec((1, SEGS), lambda k: (0, 0)),
            pl.BlockSpec((SEGS, 1), lambda k: (0, 0)),
            pl.BlockSpec((1, DEVICES * ST_DEV), lambda k: (0, 0)),
            pl.BlockSpec((1, NBAND), lambda k: (0, 0)),
        ],
        out_specs=pl.BlockSpec((DEVICES, ROWS, 128), lambda k: (0, 0, 0)),
        out_shape=jax.ShapeDtypeStruct((DEVICES, ROWS, 128), BF16),
        scratch_shapes=[
            pltpu.VMEM((128, NBAND), F32),
            pltpu.VMEM((128, NBAND), F32),
            pltpu.VMEM((64, NBAND), F32),
            pltpu.VMEM((64, NBAND), F32),
            pltpu.VMEM((512, 256), BF16),
            pltpu.VMEM((SEGS, STEP + 256), BF16),
            pltpu.VMEM((SEGS, STEP), BF16),
            pltpu.VMEM((STEP, 2 * NBAND), BF16),
            pltpu.VMEM((SEGS, 2 * NBAND), F32),
        ],
        compiler_params=pltpu.CompilerParams(vmem_limit_bytes=48 << 20),
        cost_estimate=pl.CostEstimate(
            flops=10 * SEGS * L * 512, bytes_accessed=SEGS * L * 2, transcendentals=SEGS * L
        ),
        name="transform",
    )(
        traces, traces, traces, seg_owner, seg_owner.reshape(1, SEGS), seg_slot.reshape(SEGS, 1),
        white_width.reshape(1, -1), band_bins.reshape(1, -1),
    )


def stack_kernel(half, received, spectra, wide):
    tags = received[:, 4 * CAP : 5 * CAP, :].reshape(DEVICES * CAP, 128).astype(F32)
    column = (tags[:, 0:1] * 128.0 + tags[:, 1:2] + (tags[:, 2:3] - 1.0)).astype(jnp.int32)
    total = jnp.zeros((256, ST_DEV * 128), F32)
    block = 512
    for part in range(DEVICES * CAP // block):
        sources = slice(part * block // CAP, (part + 1) * block // CAP)
        hits = column[part * block : (part + 1) * block] == iota((1, ST_DEV * 128), 1)
        hits = jnp.where(hits, 1.0, 0.0).astype(BF16)
        real = received[sources, half * CAP : half * CAP + CAP, :].reshape(block, 128)
        imag = received[sources, (2 + half) * CAP : (3 + half) * CAP, :].reshape(block, 128)
        both = jnp.concatenate([real, imag], axis=1)
        total += lax.dot_general(both, hits, (((0,), (0,)), ((), ())), preferred_element_type=F32)
    lane = iota((PAIRS, 128), 1)
    for station in range(ST_DEV):
        lanes = slice(station * 128, station * 128 + 128)
        real_first = total[0:64, lanes]
        real_second = pltpu.roll(total[64:128, lanes], 64, 1)
        imag_first = pltpu.roll(total[128:192, lanes], 96, 1)
        imag_second = pltpu.roll(total[192:256, lanes], 32, 1)
        wide[:, station, 0:128] = jnp.where(lane < 96, real_first, imag_first)
        wide[:, station, 128:256] = jnp.where(lane < 64, imag_first, real_second)
        wide[:, station, 256:384] = jnp.where(lane < 32, real_second, imag_second)
    spectra[...] = wide[...].reshape(PAIRS * ST_DEV, WIDE).astype(BF16)


def stack_half(received, half):
    return pl.pallas_call(
        functools.partial(stack_kernel, half),
        out_shape=jax.ShapeDtypeStruct((PAIRS * ST_DEV, WIDE), BF16),
        scratch_shapes=[pltpu.VMEM((PAIRS, ST_DEV, WIDE), F32)],
        compiler_params=pltpu.CompilerParams(vmem_limit_bytes=40 << 20),
        cost_estimate=pl.CostEstimate(
            flops=2 * 2048 * 1024 * 256 * 2, bytes_accessed=3 << 20, transcendentals=0
        ),
        name="stack",
    )(received)


BLOCK = 16
BLOCKS = PAIRS // BLOCK
OUT_ROWS = 16


def cross_kernel(places, *refs):
    (row_own, row_left, row_right, row_first, row_second) = refs[0:5]
    columns = refs[5:15]
    out, left, right, swapped, swap, results = refs[-6:]
    step = pl.program_id(0)

    def place(source, target, count, base):
        for block in range(2):
            at = pl.multiple_of(places[base + block] * ST_DEV, ST_DEV)
            target[:, pl.ds(at, ST_DEV), :] = (
                source[block].astype(F32).reshape(BLOCK, ST_DEV, WIDE)
            )

    @pl.when(step == 0)
    def _():
        source = iota((WIDE, WIDE), 0)
        target = iota((WIDE, WIDE), 1)
        group = (target // HOURS) % 2
        ahead = (source == target + HOURS) & (group == 0)
        behind = (source == target - HOURS) & (group == 1)
        swap[...] = (jnp.where(ahead, 1.0, 0.0) - jnp.where(behind, 1.0, 0.0)).astype(BF16)

    @pl.when(step < BLOCKS)
    def _():
        place(row_own, left, 8, 0)
        place(row_left, left, 8, 2)
        place(row_right, left, 8, 4)
        for core in range(2):
            own, one, other = columns[core * 5 : core * 5 + 3]
            place(own, right, 16, 8 + core * 8)
            place(one, right, 16, 10 + core * 8)
            place(other, right, 16, 12 + core * 8)

    @pl.when(step < BLOCKS // 2)
    def _():
        place(row_first, left, 8, 6)
        place(columns[3], right, 16, 14)
        place(columns[8], right, 16, 22)

    @pl.when((step >= BLOCKS // 2) & (step < BLOCKS))
    def _():
        place(row_second, left, 8, 6)
        place(columns[4], right, 16, 14)
        place(columns[9], right, 16, 22)

    @pl.when(step < BLOCKS)
    def _():
        plain = left[...].astype(BF16).reshape(BLOCK * 64, WIDE)
        swapped[...] = (
            jnp.dot(plain, swap[...], preferred_element_type=F32)
            .astype(BF16)
            .reshape(BLOCK, 64, WIDE)
        )
        lane = iota((1, 256), 1)
        first_mask = jnp.where(lane < 2 * HOURS, 1.0, 0.0).astype(BF16)
        second_mask = jnp.where(lane >= 2 * HOURS - 128, 1.0, 0.0).astype(BF16)

        @pl.loop(0, BLOCK)
        def _(pair):
            for part, mask in ((0, first_mask), (1, second_mask)):
                lanes = slice(part * 128, part * 128 + 256)
                rows = jnp.concatenate(
                    [left[pair, :, lanes].astype(BF16), swapped[pair, :, lanes]], axis=0
                )
                product = lax.dot_general(
                    rows * mask,
                    right[pair, :, lanes].astype(BF16),
                    (((1,), (1,)), ((), ())),
                    preferred_element_type=F32,
                )
                at = step * BLOCK + pair + part * PAIRS
                results[pl.ds(at, 128, stride=128), :] = product

    @pl.when(step >= BLOCKS)
    def _():
        first = (step - BLOCKS) * OUT_ROWS
        for row in range(OUT_ROWS):
            at = pl.multiple_of((first + row) * 128, 128)
            out[row] = results[pl.ds(at, 128), :].T.astype(BF16)


def cross_half(places, rows, columns, half, earlier):
    def whole(step):
        return (0, jnp.minimum(step, BLOCKS - 1), 0)

    def first(step):
        return (0, jnp.minimum(step, BLOCKS // 2 - 1), 0)

    def second(step):
        return (0, jnp.clip(step - BLOCKS // 2, 0, BLOCKS // 2 - 1), 0)

    shape = (2, BLOCK * ST_DEV, WIDE)
    group = [pl.BlockSpec(shape, f) for f in (whole, whole, whole, first, second)]
    per_part = 64 // OUT_ROWS

    def out_map(step):
        at = jnp.maximum(step - BLOCKS, 0)
        return (at % per_part, 0, half + 2 * (at // per_part))

    arrays = [places] + list(rows) + list(columns)
    in_specs = [pl.BlockSpec(memory_space=pltpu.SMEM)] + group * 3
    aliases = {}
    if earlier is not None:
        aliases = {len(arrays): 0}
        arrays.append(earlier)
        in_specs.append(pl.BlockSpec(memory_space=pl.ANY))
    return pl.pallas_call(
        cross_kernel,
        grid=(BLOCKS + 2 * per_part,),
        in_specs=in_specs,
        out_specs=pl.BlockSpec((OUT_ROWS, 128, 128), out_map),
        out_shape=jax.ShapeDtypeStruct((64, 128, 2 * NBAND), BF16),
        scratch_shapes=[
            pltpu.VMEM((BLOCK, 64, WIDE), F32),
            pltpu.VMEM((BLOCK, 128, WIDE), F32),
            pltpu.VMEM((BLOCK, 64, WIDE), BF16),
            pltpu.VMEM((WIDE, WIDE), BF16),
            pltpu.VMEM((128 * 128, 128), F32),
        ],
        input_output_aliases=aliases,
        compiler_params=pltpu.CompilerParams(vmem_limit_bytes=50 << 20),
        cost_estimate=pl.CostEstimate(
            flops=2 * 128 * 128 * 256 * 128 * 3, bytes_accessed=14 << 20, transcendentals=0
        ),
        name="cross",
    )(*arrays)


def ring(size, shift):
    return [(i, (i + shift) % size) for i in range(size)]


def swap_with(array, axis):
    return lax.ppermute(array, axis, [(0, 1), (1, 0)])


def spread(pair, axis):
    left = lax.ppermute(pair, axis, ring(4, 1))
    right = lax.ppermute(pair, axis, ring(4, 3))
    middle = pair.shape[1] // 2
    first = lax.ppermute(left[:, :middle], axis, ring(4, 1))
    second = lax.ppermute(right[:, middle:], axis, ring(4, 3))
    return [pair, left, right, first, second]


def block_places():
    zh, y, core, x, zl = (lax.axis_index(name) for name in AXES)
    out = []
    for shift in (0, 3, 1, 2):
        there = (x + shift) % 4
        out += [there * 2 + zl, there * 2 + (1 - zl)]
    for own in (core, 1 - core):
        for shift in (0, 3, 1, 2):
            there = (y + shift) % 4
            out += [zh * 8 + there * 2 + own, (1 - zh) * 8 + there * 2 + own]
    return jnp.stack(out).astype(jnp.int32)


def on_device(traces, seg_owner, seg_slot, white_width, band_bins):
    send = transform(traces, seg_owner, seg_slot, white_width, band_bins)
    received = lax.all_to_all(send, AXES, split_axis=0, concat_axis=0, tiled=True)
    places = block_places()
    out = None
    for half in range(2):
        own = stack_half(received, half)
        rows = spread(jnp.stack([own, swap_with(own, "zl")]), "x")
        columns = spread(jnp.stack([own, swap_with(own, "zh")]), "y")
        columns = columns + [swap_with(array, "core") for array in columns]
        out = cross_half(places, rows, columns, half, out)
    return out


def solution(mesh):
    fine = Mesh(mesh.devices.reshape(2, 4, 2, 4, 2), AXES)
    return jax.shard_map(
        on_device,
        mesh=fine,
        in_specs=(P(AXES, None), P(AXES, None), P(AXES), P(), P()),
        out_specs=P(("zh", "y", "core"), ("x", "zl"), None),
        check_vma=False,
    )
```

```python
import math

import jax
import jax.numpy as jnp
from jax import lax
from jax.experimental import pallas as pl
from jax.experimental.pallas import tpu as pltpu
from jax.sharding import Mesh, PartitionSpec as P

L = 8192
NBAND = 256
HALF = 64
WMAX = 8
ST_DEV = 8
HOURS = 96
CAP = 16
EPS = 1e-05
FLOOR = 0.5

AXES = ("zh", "y", "core", "x", "zl")
DEVICES = 128
SEGS = 512
STEP = 1024
STEPS = L // STEP
PAIRS = 64
WIDE = 4 * HOURS
TAGGED = 4 * CAP + 8
F32 = jnp.float32
BF16 = jnp.bfloat16


def iota(shape, axis):
    return lax.broadcasted_iota(jnp.int32, shape, axis)


def transform_kernel(
    main, before, after, owner_row, slot_row, width_row, bins,
    send, low_cos, low_sin, high_cos, high_sin, band, magnitude, normal, table, total,
):
    step = pl.program_id(0)

    @pl.when(step == 0)
    def _():
        unit = 2.0 * math.pi / L
        phase = (iota((128, NBAND), 0) * bins[...]) & (L - 1)
        angle = phase.astype(F32) * unit
        low_cos[...] = jnp.cos(angle)
        low_sin[...] = jnp.sin(angle)
        phase = (iota((64, NBAND), 0) * 128 * bins[...]) & (L - 1)
        angle = phase.astype(F32) * unit
        high_cos[...] = jnp.cos(angle)
        high_sin[...] = jnp.sin(angle)
        offset = iota((512, 256), 0) - 128 - iota((512, 256), 1)
        band[...] = jnp.where(jnp.abs(offset) <= HALF, 1.0, 0.0).astype(BF16)
        total[...] = jnp.zeros_like(total)

    for part in range(STEP // 128):
        high = step * (STEP // 128) + part
        cos_high = high_cos[pl.ds(high, 1), :]
        sin_high = high_sin[pl.ds(high, 1), :]
        rows = slice(part * 128, part * 128 + 128)
        table[rows, :NBAND] = (cos_high * low_cos[...] - sin_high * low_sin[...]).astype(BF16)
        table[rows, NBAND:] = (-(sin_high * low_cos[...] + cos_high * low_sin[...])).astype(BF16)

    magnitude[:, 128 : 128 + STEP] = jnp.abs(main[...])
    magnitude[:, :128] = jnp.where(step > 0, jnp.abs(before[...]), jnp.zeros((), BF16))
    magnitude[:, 128 + STEP :] = jnp.where(
        step < STEPS - 1, jnp.abs(after[...]), jnp.zeros((), BF16)
    )
    for part in range(STEP // 256):
        sums = jnp.dot(
            magnitude[:, part * 256 : part * 256 + 512], band[...], preferred_element_type=F32
        )
        place = step * STEP + part * 256 + iota((1, 256), 1)
        count = jnp.minimum(place + HALF, L - 1) - jnp.maximum(place - HALF, 0) + 1
        count = count.astype(F32)
        below = sums + count * EPS
        inverse = pl.reciprocal(below, approx=True)
        inverse = inverse * (2.0 - below * inverse)
        values = main[:, part * 256 : part * 256 + 256].astype(F32)
        normal[:, part * 256 : part * 256 + 256] = (values * (count * inverse)).astype(BF16)
    total[...] += jnp.dot(normal[...], table[...], preferred_element_type=F32)

    @pl.when(step == STEPS - 1)
    def _():
        rows = jnp.concatenate(
            [
                jnp.broadcast_to(owner_row[...].astype(F32), (64, SEGS)),
                jnp.broadcast_to(slot_row[...].astype(F32), (64, SEGS)),
            ],
            axis=0,
        )
        columns = rows.T.astype(jnp.int32)
        owner_col = columns[:, 0:1]
        slots = columns[:, 64:65]
        station = jnp.zeros_like(slots)
        for edge in range(1, ST_DEV):
            station += (slots >= edge * HOURS).astype(jnp.int32)
        hour = slots - station * HOURS
        whole = owner_col * ST_DEV + station
        hits = whole == iota((1, DEVICES * ST_DEV), 1)
        widths = jnp.sum(jnp.where(hits, width_row[...], 0).astype(F32), axis=1, keepdims=True)
        widths = widths.astype(jnp.int32)
        real = total[:, :NBAND] * (1.0 / math.sqrt(L))
        imag = total[:, NBAND:] * (1.0 / math.sqrt(L))
        amplitude = jnp.sqrt(real * real + imag * imag)
        lane = iota((1, NBAND), 1)
        smooth = amplitude
        for width in range(1, WMAX + 1):
            up = pltpu.roll(amplitude, width, 1)
            down = pltpu.roll(amplitude, NBAND - width, 1)
            both = jnp.where(lane >= width, up, 0.0) + jnp.where(lane < NBAND - width, down, 0.0)
            smooth += jnp.where(widths >= width, both, 0.0)
        number = jnp.minimum(lane + widths, NBAND - 1) - jnp.maximum(lane - widths, 0) + 1
        factor = 1.0 / jnp.maximum(smooth / number.astype(F32), FLOOR)
        lanes = iota((SEGS, 128), 1)
        extra = jnp.where(
            lanes == 0, station, jnp.where(lanes == 1, hour, jnp.where(lanes == 2, 1, 0))
        )
        whitened = jnp.concatenate(
            [
                (real * factor).astype(BF16),
                (imag * factor).astype(BF16),
                extra.astype(F32).astype(BF16),
            ],
            axis=1,
        )
        same = (owner_col == owner_row[...]) & (iota((SEGS, SEGS), 0) < iota((SEGS, SEGS), 1))
        rank = jnp.sum(same.astype(F32), axis=0, keepdims=True).astype(jnp.int32)
        target = owner_row[...] * CAP + rank
        for part in range(4):
            chosen = target == iota((512, SEGS), 0) + part * 512
            chosen = jnp.where(chosen, 1.0, 0.0).astype(BF16)
            picked = jnp.dot(chosen, whitened, preferred_element_type=F32)
            tags = picked[:, 2 * NBAND :].reshape(32, CAP, 128)
            tags = tags[:, :8] + pltpu.roll(tags[:, 8:], 64, 2)
            send[part * 32 : part * 32 + 32, 4 * CAP :, :] = tags.astype(BF16)
            picked = picked.astype(BF16)
            for tile in range(4):
                send[part * 32 : part * 32 + 32, tile * CAP : tile * CAP + CAP, :] = picked[
                    :, tile * 128 : tile * 128 + 128
                ].reshape(32, CAP, 128)


def transform(traces, seg_owner, seg_slot, white_width, band_bins):
    return pl.pallas_call(
        transform_kernel,
        grid=(STEPS,),
        in_specs=[
            pl.BlockSpec((SEGS, STEP), lambda k: (0, k)),
            pl.BlockSpec((SEGS, 128), lambda k: (0, jnp.maximum(k * (STEP // 128) - 1, 0))),
            pl.BlockSpec(
                (SEGS, 128), lambda k: (0, jnp.minimum((k + 1) * (STEP // 128), L // 128 - 1))
            ),
            pl.BlockSpec((1, SEGS), lambda k: (0, 0)),
            pl.BlockSpec((1, SEGS), lambda k: (0, 0)),
            pl.BlockSpec((1, DEVICES * ST_DEV), lambda k: (0, 0)),
            pl.BlockSpec((1, NBAND), lambda k: (0, 0)),
        ],
        out_specs=pl.BlockSpec((DEVICES, TAGGED, 128), lambda k: (0, 0, 0)),
        out_shape=jax.ShapeDtypeStruct((DEVICES, TAGGED, 128), BF16),
        scratch_shapes=[
            pltpu.VMEM((128, NBAND), F32),
            pltpu.VMEM((128, NBAND), F32),
            pltpu.VMEM((64, NBAND), F32),
            pltpu.VMEM((64, NBAND), F32),
            pltpu.VMEM((512, 256), BF16),
            pltpu.VMEM((SEGS, STEP + 256), BF16),
            pltpu.VMEM((SEGS, STEP), BF16),
            pltpu.VMEM((STEP, 2 * NBAND), BF16),
            pltpu.VMEM((SEGS, 2 * NBAND), F32),
        ],
        compiler_params=pltpu.CompilerParams(vmem_limit_bytes=58 << 20),
        cost_estimate=pl.CostEstimate(
            flops=10 * SEGS * L * 512, bytes_accessed=SEGS * L * 2, transcendentals=SEGS * L
        ),
        name="transform",
    )(
        traces, traces, traces, seg_owner.reshape(1, SEGS), seg_slot.reshape(1, SEGS),
        white_width.reshape(1, -1), band_bins.reshape(1, -1),
    )


def stack_kernel(received, spectra, wide):
    half = pl.program_id(0)
    tags = received[:, 4 * CAP :, :].astype(F32)
    tags = jnp.concatenate([tags, pltpu.roll(tags, 64, 2)], axis=1).reshape(DEVICES * CAP, 128)
    column = (tags[:, 0:1] * 128.0 + tags[:, 1:2] + (tags[:, 2:3] - 1.0)).astype(jnp.int32)
    total = jnp.zeros((256, ST_DEV * 128), F32)
    block = 512
    at = pl.multiple_of(half * CAP, CAP)
    for part in range(DEVICES * CAP // block):
        sources = slice(part * block // CAP, (part + 1) * block // CAP)
        hits = column[part * block : (part + 1) * block] == iota((1, ST_DEV * 128), 1)
        hits = jnp.where(hits, 1.0, 0.0).astype(BF16)
        real = received[sources, pl.ds(at, CAP), :].reshape(block, 128)
        imag = received[sources, pl.ds(at + 2 * CAP, CAP), :].reshape(block, 128)
        both = jnp.concatenate([real, imag], axis=1)
        total += lax.dot_general(both, hits, (((0,), (0,)), ((), ())), preferred_element_type=F32)
    lane = iota((PAIRS, 128), 1)
    for station in range(ST_DEV):
        lanes = slice(station * 128, station * 128 + 128)
        real_first = total[0:64, lanes]
        real_second = pltpu.roll(total[64:128, lanes], 64, 1)
        imag_first = pltpu.roll(total[128:192, lanes], 96, 1)
        imag_second = pltpu.roll(total[192:256, lanes], 32, 1)
        wide[:, station, 0:128] = jnp.where(lane < 96, real_first, imag_first)
        wide[:, station, 128:256] = jnp.where(lane < 64, imag_first, real_second)
        wide[:, station, 256:384] = jnp.where(lane < 32, real_second, imag_second)
    spectra[...] = wide[...].reshape(PAIRS * ST_DEV, WIDE).astype(BF16)


def stack(received):
    return pl.pallas_call(
        stack_kernel,
        grid=(2,),
        in_specs=[pl.BlockSpec((DEVICES, TAGGED, 128), lambda k: (0, 0, 0))],
        out_specs=pl.BlockSpec((PAIRS * ST_DEV, WIDE), lambda k: (k, 0)),
        out_shape=jax.ShapeDtypeStruct((2 * PAIRS * ST_DEV, WIDE), BF16),
        scratch_shapes=[pltpu.VMEM((PAIRS, ST_DEV, WIDE), F32)],
        compiler_params=pltpu.CompilerParams(vmem_limit_bytes=20 << 20),
        cost_estimate=pl.CostEstimate(
            flops=2 * 2048 * 1024 * 256 * 2, bytes_accessed=3 << 20, transcendentals=0
        ),
        name="stack",
    )(received)


BLOCK = 32
BLOCKS = PAIRS // BLOCK
OUT_ROWS = 16
STRIDE = 2 * 2 * PAIRS + 8


def cross_kernel(places, *refs):
    rows, columns = refs[0:8], list(refs[8:16])
    early, late, beside_left, beside_far = refs[16:20]
    out, row_blocks, column_blocks, left, right, swapped, swap, results, arrived = refs[20:]
    columns += [early.at[0], early.at[1], early.at[2], beside_left]
    columns += [early.at[3], late.at[1], late.at[0], beside_far]
    step = pl.program_id(0)

    def copies(block):
        size = BLOCK * ST_DEV
        at = pl.ds(pl.multiple_of(block * size, size), size)
        out = []
        for index in range(24):
            if index < 8:
                source, target = rows[index], row_blocks
            else:
                source, target = columns[index - 8], column_blocks
            out.append(
                pltpu.make_async_copy(
                    source.at[at], target.at[places[index], at], arrived.at[block, index]
                )
            )
        return out

    @pl.when(step == 0)
    def _():
        @pl.loop(0, 2 * BLOCKS)
        def _(block):
            for copy in copies(block):
                copy.start()

    @pl.when(step < 2 * BLOCKS)
    def _():
        for copy in copies(step):
            copy.wait()

    @pl.when(step == 0)
    def _():
        source = iota((WIDE, WIDE), 0)
        target = iota((WIDE, WIDE), 1)
        group = (target // HOURS) % 2
        ahead = (source == target + HOURS) & (group == 0)
        behind = (source == target - HOURS) & (group == 1)
        swap[...] = (jnp.where(ahead, 1.0, 0.0) - jnp.where(behind, 1.0, 0.0)).astype(BF16)

    @pl.when(step < 2 * BLOCKS)
    def _():
        size = BLOCK * ST_DEV
        whole = pl.ds(pl.multiple_of(step * size, size), size)
        for blocks, target, count in ((row_blocks, left, 8), (column_blocks, right, 16)):
            for index in range(0, count, 2):
                both = [
                    blocks[index + k, whole, :].astype(F32).reshape(BLOCK, ST_DEV, WIDE)
                    for k in range(2)
                ]
                target[:, index * ST_DEV : (index + 2) * ST_DEV, :] = jnp.concatenate(
                    both, axis=1
                ).astype(BF16)
        plain = left[...].reshape(BLOCK * 64, WIDE)
        swapped[...] = (
            jnp.dot(plain, swap[...], preferred_element_type=F32)
            .astype(BF16)
            .reshape(BLOCK, 64, WIDE)
        )
        lane = iota((1, 256), 1)
        first_mask = jnp.where(lane < 2 * HOURS, 1.0, 0.0).astype(BF16)
        second_mask = jnp.where(lane >= 2 * HOURS - 128, 1.0, 0.0).astype(BF16)

        @pl.loop(0, BLOCK, unroll=32)
        def _(pair):
            for part, mask in ((0, first_mask), (1, second_mask)):
                lanes = slice(part * 128, part * 128 + 256)
                rows = jnp.concatenate(
                    [left[pair, :, lanes], swapped[pair, :, lanes]], axis=0
                )
                product = lax.dot_general(
                    rows * mask,
                    right[pair, :, lanes],
                    (((1,), (1,)), ((), ())),
                    preferred_element_type=F32,
                )
                at = step * BLOCK + (step // BLOCKS) * PAIRS + pair + part * PAIRS
                results[pl.ds(at, 128, stride=STRIDE), :] = product

    @pl.when(step >= 2 * BLOCKS)
    def _():
        first = (step - 2 * BLOCKS) * OUT_ROWS
        for row in range(OUT_ROWS):
            for part in range(2):
                for half in range(2):
                    at = (first + row + part * 64) * STRIDE + half * 128
                    lanes = slice(part * NBAND + half * 128, part * NBAND + half * 128 + 128)
                    product = results[pl.ds(pl.multiple_of(at, 8), 128), :]
                    out[row, :, lanes] = product.T.astype(BF16)


def cross(places, rows, columns):
    return pl.pallas_call(
        cross_kernel,
        grid=(2 * BLOCKS + 64 // OUT_ROWS,),
        in_specs=[pl.BlockSpec(memory_space=pltpu.SMEM)] + [pl.BlockSpec(memory_space=pltpu.HBM)] * 20,
        out_specs=pl.BlockSpec(
            (OUT_ROWS, 128, 2 * NBAND), lambda step: (jnp.maximum(step - 2 * BLOCKS, 0), 0, 0)
        ),
        out_shape=jax.ShapeDtypeStruct((64, 128, 2 * NBAND), BF16),
        scratch_shapes=[
            pltpu.VMEM((8, 2 * PAIRS * ST_DEV, WIDE), BF16),
            pltpu.VMEM((16, 2 * PAIRS * ST_DEV, WIDE), BF16),
            pltpu.VMEM((BLOCK, 64, WIDE), BF16),
            pltpu.VMEM((BLOCK, 128, WIDE), BF16),
            pltpu.VMEM((BLOCK, 64, WIDE), BF16),
            pltpu.VMEM((WIDE, WIDE), BF16),
            pltpu.VMEM((128 * STRIDE, 128), F32),
            pltpu.SemaphoreType.DMA((2 * BLOCKS, 24)),
        ],
        compiler_params=pltpu.CompilerParams(vmem_limit_bytes=58 << 20),
        cost_estimate=pl.CostEstimate(
            flops=2 * 128 * 128 * 256 * 128 * 3, bytes_accessed=14 << 20, transcendentals=0
        ),
        name="cross",
    )(places, *rows, *columns)


def ring(size, shift):
    return [(i, (i + shift) % size) for i in range(size)]


def turn(moves, *others):
    arrays = [move[0] for move in moves]
    arrays = lax.optimization_barrier(tuple(arrays) + others)[: len(moves)]
    return [lax.ppermute(array, axis, pairs) for array, (_, axis, pairs) in zip(arrays, moves)]


UP, DOWN, SWAP = ring(4, 1), ring(4, 3), [(0, 1), (1, 0)]


def gather(own):
    lx, rx, ly, ry, q = turn(
        [(own, "x", UP), (own, "x", DOWN), (own, "y", UP), (own, "y", DOWN), (own, "zh", SWAP)]
    )
    early = jnp.stack([own, q, ly, ry])
    fx, fy, rq, p, s_early = turn(
        [(lx, "x", UP), (ly, "y", UP), (q, "y", DOWN), (own, "zl", SWAP), (early, "core", SWAP)],
        rx,
    )
    late = jnp.stack([fy, rq])
    lp, rp, lq, gq, gp = turn(
        [(p, "x", UP), (p, "x", DOWN), (q, "y", UP), (rq, "y", DOWN), (fx, "zl", SWAP)],
        fy, s_early,
    )
    s_late, s_lq, s_gq = turn(
        [(late, "core", SWAP), (lq, "core", SWAP), (gq, "core", SWAP)], lp, rp, gp
    )
    rows = [own, p, lx, lp, rx, rp, fx, gp]
    columns = [own, q, ly, lq, ry, rq, fy, gq, s_early, s_late, s_lq, s_gq]
    return rows, columns


def block_places():
    zh, y, core, x, zl = (lax.axis_index(name) for name in AXES)
    out = []
    for shift in (0, 3, 1, 2):
        there = (x + shift) % 4
        out += [there * 2 + zl, there * 2 + (1 - zl)]
    for own in (core, 1 - core):
        for shift in (0, 3, 1, 2):
            there = (y + shift) % 4
            out += [zh * 8 + there * 2 + own, (1 - zh) * 8 + there * 2 + own]
    return jnp.stack(out).astype(jnp.int32)


def on_device(traces, seg_owner, seg_slot, white_width, band_bins):
    send = transform(traces, seg_owner, seg_slot, white_width, band_bins)
    places = block_places()
    received = lax.all_to_all(send, AXES, split_axis=0, concat_axis=0, tiled=True)
    own = stack(received)
    rows, columns = gather(own)
    return cross(places, rows, columns)


def solution(mesh):
    fine = Mesh(mesh.devices.reshape(2, 4, 2, 4, 2), AXES)
    return jax.shard_map(
        on_device,
        mesh=fine,
        in_specs=(P(AXES, None), P(AXES, None), P(AXES), P(), P()),
        out_specs=P(("zh", "y", "core"), ("x", "zl"), None),
        check_vma=False,
    )
```

```python
import math

import jax
import jax.numpy as jnp
from jax import lax
from jax.experimental import pallas as pl
from jax.experimental.pallas import tpu as pltpu
from jax.sharding import Mesh, PartitionSpec as P

L = 8192
NBAND = 256
HALF = 64
WMAX = 8
ST_DEV = 8
HOURS = 96
CAP = 16
EPS = 1e-05
FLOOR = 0.5

AXES = ("zh", "y", "core", "x", "zl")
DEVICES = 128
SEGS = 512
STEP = 2048
STEPS = L // STEP
PAIRS = 64
WIDE = 4 * HOURS
TAGGED = 4 * CAP + 8
F32 = jnp.float32
BF16 = jnp.bfloat16


def iota(shape, axis):
    return lax.broadcasted_iota(jnp.int32, shape, axis)


def transform_kernel(
    main, before, after, owner_row, slot_row, width_row, bins,
    send, low_cos, low_sin, high_cos, high_sin, band, magnitude, normal, table, total,
):
    step = pl.program_id(0)

    @pl.when(step == 0)
    def _():
        unit = 2.0 * math.pi / L
        phase = (iota((128, NBAND), 0) * bins[...]) & (L - 1)
        angle = phase.astype(F32) * unit
        low_cos[...] = jnp.cos(angle)
        low_sin[...] = jnp.sin(angle)
        phase = (iota((64, NBAND), 0) * 128 * bins[...]) & (L - 1)
        angle = phase.astype(F32) * unit
        high_cos[...] = jnp.cos(angle)
        high_sin[...] = jnp.sin(angle)
        offset = iota((512, 256), 0) - 128 - iota((512, 256), 1)
        band[...] = jnp.where(jnp.abs(offset) <= HALF, 1.0, 0.0).astype(BF16)
        total[...] = jnp.zeros_like(total)

    for part in range(STEP // 128):
        high = step * (STEP // 128) + part
        cos_high = high_cos[pl.ds(high, 1), :]
        sin_high = high_sin[pl.ds(high, 1), :]
        rows = slice(part * 128, part * 128 + 128)
        table[rows, :NBAND] = (cos_high * low_cos[...] - sin_high * low_sin[...]).astype(BF16)
        table[rows, NBAND:] = (-(sin_high * low_cos[...] + cos_high * low_sin[...])).astype(BF16)

    magnitude[:, 128 : 128 + STEP] = jnp.abs(main[...])
    magnitude[:, :128] = jnp.where(step > 0, jnp.abs(before[...]), jnp.zeros((), BF16))
    magnitude[:, 128 + STEP :] = jnp.where(
        step < STEPS - 1, jnp.abs(after[...]), jnp.zeros((), BF16)
    )
    for part in range(STEP // 256):
        sums = jnp.dot(
            magnitude[:, part * 256 : part * 256 + 512], band[...], preferred_element_type=F32
        )
        place = step * STEP + part * 256 + iota((1, 256), 1)
        count = jnp.minimum(place + HALF, L - 1) - jnp.maximum(place - HALF, 0) + 1
        count = count.astype(F32)
        below = sums + count * EPS
        inverse = pl.reciprocal(below, approx=True)
        values = main[:, part * 256 : part * 256 + 256].astype(F32)
        normal[:, part * 256 : part * 256 + 256] = (values * (count * inverse)).astype(BF16)
    total[...] += jnp.dot(normal[...], table[...], preferred_element_type=F32)

    @pl.when(step == STEPS - 1)
    def _():
        rows = jnp.concatenate(
            [
                jnp.broadcast_to(owner_row[...].astype(F32), (64, SEGS)),
                jnp.broadcast_to(slot_row[...].astype(F32), (64, SEGS)),
            ],
            axis=0,
        )
        columns = rows.T.astype(jnp.int32)
        owner_col = columns[:, 0:1]
        slots = columns[:, 64:65]
        station = jnp.zeros_like(slots)
        for edge in range(1, ST_DEV):
            station += (slots >= edge * HOURS).astype(jnp.int32)
        hour = slots - station * HOURS
        whole = owner_col * ST_DEV + station
        hits = whole == iota((1, DEVICES * ST_DEV), 1)
        widths = jnp.sum(jnp.where(hits, width_row[...].astype(F32), 0.0), axis=1, keepdims=True)
        widths = widths.astype(jnp.int32)
        real = total[:, :NBAND] * (1.0 / math.sqrt(L))
        imag = total[:, NBAND:] * (1.0 / math.sqrt(L))
        amplitude = jnp.sqrt(real * real + imag * imag)
        lane = iota((1, NBAND), 1)
        smooth = amplitude
        for width in range(1, WMAX + 1):
            up = pltpu.roll(amplitude, width, 1)
            down = pltpu.roll(amplitude, NBAND - width, 1)
            both = jnp.where(lane >= width, up, 0.0) + jnp.where(lane < NBAND - width, down, 0.0)
            smooth += jnp.where(widths >= width, both, 0.0)
        number = jnp.minimum(lane + widths, NBAND - 1) - jnp.maximum(lane - widths, 0) + 1
        factor = 1.0 / jnp.maximum(smooth / number.astype(F32), FLOOR)
        lanes = iota((SEGS, 128), 1)
        extra = jnp.where(
            lanes == 0, station, jnp.where(lanes == 1, hour, jnp.where(lanes == 2, 1, 0))
        )
        whitened = jnp.concatenate(
            [
                (real * factor).astype(BF16),
                (imag * factor).astype(BF16),
                extra.astype(F32).astype(BF16),
            ],
            axis=1,
        )
        same = (owner_col == owner_row[...]) & (iota((SEGS, SEGS), 0) < iota((SEGS, SEGS), 1))
        rank = jnp.sum(same.astype(F32), axis=0, keepdims=True).astype(jnp.int32)
        target = owner_row[...] * CAP + rank
        for part in range(4):
            chosen = target == iota((512, SEGS), 0) + part * 512
            chosen = jnp.where(chosen, 1.0, 0.0).astype(BF16)
            picked = jnp.dot(chosen, whitened, preferred_element_type=F32)
            tags = picked[:, 2 * NBAND :].reshape(32, CAP, 128)
            tags = tags[:, :8] + pltpu.roll(tags[:, 8:], 64, 2)
            send[part * 32 : part * 32 + 32, 4 * CAP :, :] = tags.astype(BF16)
            picked = picked.astype(BF16)
            for tile in range(4):
                send[part * 32 : part * 32 + 32, tile * CAP : tile * CAP + CAP, :] = picked[
                    :, tile * 128 : tile * 128 + 128
                ].reshape(32, CAP, 128)


def transform(traces, seg_owner, seg_slot, white_width, band_bins):
    return pl.pallas_call(
        transform_kernel,
        grid=(STEPS,),
        in_specs=[
            pl.BlockSpec((SEGS, STEP), lambda k: (0, k)),
            pl.BlockSpec((SEGS, 128), lambda k: (0, jnp.maximum(k * (STEP // 128) - 1, 0))),
            pl.BlockSpec(
                (SEGS, 128), lambda k: (0, jnp.minimum((k + 1) * (STEP // 128), L // 128 - 1))
            ),
            pl.BlockSpec((1, SEGS), lambda k: (0, 0)),
            pl.BlockSpec((1, SEGS), lambda k: (0, 0)),
            pl.BlockSpec((1, DEVICES * ST_DEV), lambda k: (0, 0)),
            pl.BlockSpec((1, NBAND), lambda k: (0, 0)),
        ],
        out_specs=pl.BlockSpec((DEVICES, TAGGED, 128), lambda k: (0, 0, 0)),
        out_shape=jax.ShapeDtypeStruct((DEVICES, TAGGED, 128), BF16),
        scratch_shapes=[
            pltpu.VMEM((128, NBAND), F32),
            pltpu.VMEM((128, NBAND), F32),
            pltpu.VMEM((64, NBAND), F32),
            pltpu.VMEM((64, NBAND), F32),
            pltpu.VMEM((512, 256), BF16),
            pltpu.VMEM((SEGS, STEP + 256), BF16),
            pltpu.VMEM((SEGS, STEP), BF16),
            pltpu.VMEM((STEP, 2 * NBAND), BF16),
            pltpu.VMEM((SEGS, 2 * NBAND), F32),
        ],
        compiler_params=pltpu.CompilerParams(vmem_limit_bytes=58 << 20),
        cost_estimate=pl.CostEstimate(
            flops=10 * SEGS * L * 512, bytes_accessed=SEGS * L * 2, transcendentals=SEGS * L
        ),
        name="transform",
    )(
        traces, traces, traces, seg_owner.reshape(1, SEGS), seg_slot.reshape(1, SEGS),
        white_width.reshape(1, -1), band_bins.reshape(1, -1),
    )


def stack_kernel(received, spectra, wide):
    tags = received[:, 4 * CAP :, :].astype(F32)
    tags = jnp.concatenate([tags, pltpu.roll(tags, 64, 2)], axis=1).reshape(DEVICES * CAP, 128)
    column = (tags[:, 0:1] * 128.0 + tags[:, 1:2] + (tags[:, 2:3] - 1.0)).astype(jnp.int32)
    total = None
    block = 512
    for part in range(DEVICES * CAP // block):
        sources = slice(part * block // CAP, (part + 1) * block // CAP)
        hits = column[part * block : (part + 1) * block] == iota((1, ST_DEV * 128), 1)
        hits = jnp.where(hits, 1.0, 0.0).astype(BF16)
        values = jnp.concatenate(
            [
                received[sources, tile * CAP : tile * CAP + CAP, :].reshape(block, 128)
                for tile in range(4)
            ],
            axis=1,
        )
        term = lax.dot_general(values, hits, (((0,), (0,)), ((), ())), preferred_element_type=F32)
        total = term if total is None else total + term
    lane = iota((PAIRS, 128), 1)
    for half in range(2):
        rows = half * 128
        for station in range(ST_DEV):
            lanes = slice(station * 128, station * 128 + 128)
            real_first = total[rows : rows + 64, lanes]
            real_second = pltpu.roll(total[rows + 64 : rows + 128, lanes], 64, 1)
            imag_first = pltpu.roll(total[rows + 256 : rows + 320, lanes], 96, 1)
            imag_second = pltpu.roll(total[rows + 320 : rows + 384, lanes], 32, 1)
            wide[:, station, 0:128] = jnp.where(lane < 96, real_first, imag_first)
            wide[:, station, 128:256] = jnp.where(lane < 64, imag_first, real_second)
            wide[:, station, 256:384] = jnp.where(lane < 32, real_second, imag_second)
        spectra[half * PAIRS * ST_DEV : (half + 1) * PAIRS * ST_DEV] = (
            wide[...].reshape(PAIRS * ST_DEV, WIDE).astype(BF16)
        )


def stack(received):
    return pl.pallas_call(
        stack_kernel,
        out_shape=jax.ShapeDtypeStruct((2 * PAIRS * ST_DEV, WIDE), BF16),
        scratch_shapes=[pltpu.VMEM((PAIRS, ST_DEV, WIDE), F32)],
        compiler_params=pltpu.CompilerParams(vmem_limit_bytes=40 << 20),
        cost_estimate=pl.CostEstimate(
            flops=2 * 2048 * 1024 * 256 * 2, bytes_accessed=3 << 20, transcendentals=0
        ),
        name="stack",
    )(received)


BLOCK = 32
BLOCKS = PAIRS // BLOCK
OUT_ROWS = 16
STRIDE = 2 * 2 * PAIRS + 8


def cross_kernel(places, *refs):
    rows, columns = refs[0:8], list(refs[8:16])
    early, late, beside_left, beside_far = refs[16:20]
    out, row_blocks, column_blocks, left, right, swapped, swap, results, arrived = refs[20:]
    columns += [early.at[0], early.at[1], early.at[2], beside_left]
    columns += [early.at[3], late.at[1], late.at[0], beside_far]
    step = pl.program_id(0)

    def copies(block):
        size = BLOCK * ST_DEV
        at = pl.ds(pl.multiple_of(block * size, size), size)
        out = []
        for index in range(24):
            if index < 8:
                source, target = rows[index], row_blocks
            else:
                source, target = columns[index - 8], column_blocks
            out.append(
                pltpu.make_async_copy(
                    source.at[at], target.at[places[index], at], arrived.at[block, index]
                )
            )
        return out

    @pl.when(step == 0)
    def _():
        @pl.loop(0, 2 * BLOCKS)
        def _(block):
            for copy in copies(block):
                copy.start()

        for part in range(2):
            source = iota((256, 256), 0) + part * 128
            target = iota((256, 256), 1) + part * 128
            mine = target // (2 * HOURS) == part
            group = (target // HOURS) % 2
            ahead = mine & (source == target + HOURS) & (group == 0)
            behind = mine & (source == target - HOURS) & (group == 1)
            swap[part] = (jnp.where(ahead, 1.0, 0.0) - jnp.where(behind, 1.0, 0.0)).astype(BF16)

    @pl.when(step < 2 * BLOCKS)
    def _():
        for copy in copies(step):
            copy.wait()

    @pl.when(step < 2 * BLOCKS)
    def _():
        size = BLOCK * ST_DEV
        whole = pl.ds(pl.multiple_of(step * size, size), size)
        for blocks, target, count in ((row_blocks, left, 8), (column_blocks, right, 16)):
            for index in range(0, count, 2):
                both = [
                    blocks[index + k, whole, :].astype(F32).reshape(BLOCK, ST_DEV, WIDE)
                    for k in range(2)
                ]
                target[:, index * ST_DEV : (index + 2) * ST_DEV, :] = jnp.concatenate(
                    both, axis=1
                ).astype(BF16)
        plain = left[...].reshape(BLOCK * 64, WIDE)
        for part in range(2):
            lanes = slice(part * 128, part * 128 + 256)
            swapped[part] = (
                jnp.dot(plain[:, lanes], swap[part], preferred_element_type=F32)
                .astype(BF16)
                .reshape(BLOCK, 64, 256)
            )
        lane = iota((1, 256), 1)
        first_mask = jnp.where(lane < 2 * HOURS, 1.0, 0.0).astype(BF16)
        second_mask = jnp.where(lane >= 2 * HOURS - 128, 1.0, 0.0).astype(BF16)

        @pl.loop(0, BLOCK, unroll=32)
        def _(pair):
            for part, mask in ((0, first_mask), (1, second_mask)):
                lanes = slice(part * 128, part * 128 + 256)
                rows = jnp.concatenate([left[pair, :, lanes] * mask, swapped[part, pair]], axis=0)
                product = lax.dot_general(
                    rows,
                    right[pair, :, lanes],
                    (((1,), (1,)), ((), ())),
                    preferred_element_type=F32,
                )
                at = step * BLOCK + (step // BLOCKS) * PAIRS + pair + part * PAIRS
                results[pl.ds(at, 128, stride=STRIDE), :] = product

    @pl.when(step >= 2 * BLOCKS)
    def _():
        first = (step - 2 * BLOCKS) * OUT_ROWS
        for row in range(OUT_ROWS):
            for part in range(2):
                for half in range(2):
                    at = (first + row + part * 64) * STRIDE + half * 128
                    lanes = slice(part * NBAND + half * 128, part * NBAND + half * 128 + 128)
                    product = results[pl.ds(pl.multiple_of(at, 8), 128), :]
                    out[row, :, lanes] = product.T.astype(BF16)


def cross(places, rows, columns):
    return pl.pallas_call(
        cross_kernel,
        grid=(2 * BLOCKS + 64 // OUT_ROWS,),
        in_specs=[pl.BlockSpec(memory_space=pltpu.SMEM)] + [pl.BlockSpec(memory_space=pltpu.HBM)] * 20,
        out_specs=pl.BlockSpec(
            (OUT_ROWS, 128, 2 * NBAND), lambda step: (jnp.maximum(step - 2 * BLOCKS, 0), 0, 0)
        ),
        out_shape=jax.ShapeDtypeStruct((64, 128, 2 * NBAND), BF16),
        scratch_shapes=[
            pltpu.VMEM((8, 2 * PAIRS * ST_DEV, WIDE), BF16),
            pltpu.VMEM((16, 2 * PAIRS * ST_DEV, WIDE), BF16),
            pltpu.VMEM((BLOCK, 64, WIDE), BF16),
            pltpu.VMEM((BLOCK, 128, WIDE), BF16),
            pltpu.VMEM((2, BLOCK, 64, 256), BF16),
            pltpu.VMEM((2, 256, 256), BF16),
            pltpu.VMEM((128 * STRIDE, 128), F32),
            pltpu.SemaphoreType.DMA((2 * BLOCKS, 24)),
        ],
        compiler_params=pltpu.CompilerParams(vmem_limit_bytes=58 << 20),
        cost_estimate=pl.CostEstimate(
            flops=2 * 128 * 128 * 256 * 128 * 3, bytes_accessed=14 << 20, transcendentals=0
        ),
        name="cross",
    )(places, *rows, *columns)


def ring(size, shift):
    return [(i, (i + shift) % size) for i in range(size)]


def move(array, axis, pairs, *others):
    return lax.ppermute(lax.optimization_barrier((array,) + others)[0], axis, pairs)


UP, DOWN, SWAP = ring(4, 1), ring(4, 3), [(0, 1), (1, 0)]


def gather(own):
    q = move(own, "zh", SWAP)
    lx, rx = move(own, "x", UP), move(own, "x", DOWN)
    ly, ry = move(own, "y", UP), move(own, "y", DOWN)
    p = move(own, "zl", SWAP, ly, ry)
    fx = move(lx, "x", UP, rx)
    fy, rq = move(ly, "y", UP, ry), move(q, "y", DOWN, ry)
    s_early = move(jnp.stack([own, q, ly, ry]), "core", SWAP, lx, rx)
    lp, rp = move(p, "x", UP, fx), move(p, "x", DOWN, fx)
    lq, gq = move(q, "y", UP, fy, rq), move(rq, "y", DOWN, fy)
    gp = move(fx, "zl", SWAP, p, s_early)
    s_late = move(jnp.stack([fy, rq]), "core", SWAP, s_early, lp, rp)
    s_lq = move(lq, "core", SWAP, gp)
    s_gq = move(gq, "core", SWAP, gp)
    rows = [own, p, lx, lp, rx, rp, fx, gp]
    columns = [own, q, ly, lq, ry, rq, fy, gq, s_early, s_late, s_lq, s_gq]
    return rows, columns


def block_places():
    zh, y, core, x, zl = (lax.axis_index(name) for name in AXES)
    out = []
    for shift in (0, 3, 1, 2):
        there = (x + shift) % 4
        out += [there * 2 + zl, there * 2 + (1 - zl)]
    for own in (core, 1 - core):
        for shift in (0, 3, 1, 2):
            there = (y + shift) % 4
            out += [zh * 8 + there * 2 + own, (1 - zh) * 8 + there * 2 + own]
    return jnp.stack(out).astype(jnp.int32)


def on_device(traces, seg_owner, seg_slot, white_width, band_bins):
    send = transform(traces, seg_owner, seg_slot, white_width, band_bins)
    places = block_places()
    received = lax.all_to_all(send, AXES, split_axis=0, concat_axis=0, tiled=True)
    own = stack(received)
    rows, columns = gather(own)
    return cross(places, rows, columns)


def solution(mesh):
    fine = Mesh(mesh.devices.reshape(2, 4, 2, 4, 2), AXES)
    return jax.shard_map(
        on_device,
        mesh=fine,
        in_specs=(P(AXES, None), P(AXES, None), P(AXES), P(), P()),
        out_specs=P(("zh", "y", "core"), ("x", "zl"), None),
        check_vma=False,
    )
```

```python
import math

import jax
import jax.numpy as jnp
from jax import lax
from jax.experimental import pallas as pl
from jax.experimental.pallas import tpu as pltpu
from jax.sharding import Mesh, PartitionSpec as P

L = 8192
NBAND = 256
HALF = 64
WMAX = 8
ST_DEV = 8
HOURS = 96
CAP = 16
EPS = 1e-05
FLOOR = 0.5

AXES = ("zh", "y", "core", "x", "zl")
DEVICES = 128
SEGS = 512
STEP = 2048
STEPS = L // STEP
PAIRS = 64
WIDE = 4 * HOURS
TAGGED = 4 * CAP + 8
F32 = jnp.float32
BF16 = jnp.bfloat16


def iota(shape, axis):
    return lax.broadcasted_iota(jnp.int32, shape, axis)


def transform_kernel(
    main, before, after, owner_row, slot_row, width_row, bins,
    send, low_cos, low_sin, high_cos, high_sin, band, magnitude, normal, table, total,
):
    step = pl.program_id(0)

    @pl.when(step == 0)
    def _():
        unit = 2.0 * math.pi / L
        phase = (iota((128, NBAND), 0) * bins[...]) & (L - 1)
        angle = phase.astype(F32) * unit
        low_cos[...] = jnp.cos(angle)
        low_sin[...] = jnp.sin(angle)
        phase = (iota((64, NBAND), 0) * 128 * bins[...]) & (L - 1)
        angle = phase.astype(F32) * unit
        high_cos[...] = jnp.cos(angle)
        high_sin[...] = jnp.sin(angle)
        offset = iota((512, 256), 0) - 128 - iota((512, 256), 1)
        band[...] = jnp.where(jnp.abs(offset) <= HALF, 1.0, 0.0).astype(BF16)
        total[...] = jnp.zeros_like(total)

    for part in range(STEP // 128):
        high = step * (STEP // 128) + part
        cos_high = high_cos[pl.ds(high, 1), :]
        sin_high = high_sin[pl.ds(high, 1), :]
        rows = slice(part * 128, part * 128 + 128)
        table[rows, :NBAND] = (cos_high * low_cos[...] - sin_high * low_sin[...]).astype(BF16)
        table[rows, NBAND:] = (-(sin_high * low_cos[...] + cos_high * low_sin[...])).astype(BF16)

    magnitude[:, 128 : 128 + STEP] = jnp.abs(main[...])
    magnitude[:, :128] = jnp.where(step > 0, jnp.abs(before[...]), jnp.zeros((), BF16))
    magnitude[:, 128 + STEP :] = jnp.where(
        step < STEPS - 1, jnp.abs(after[...]), jnp.zeros((), BF16)
    )
    for part in range(STEP // 256):
        sums = jnp.dot(
            magnitude[:, part * 256 : part * 256 + 512], band[...], preferred_element_type=F32
        )
        place = step * STEP + part * 256 + iota((1, 256), 1)
        count = jnp.minimum(place + HALF, L - 1) - jnp.maximum(place - HALF, 0) + 1
        count = count.astype(F32)
        below = sums + count * EPS
        inverse = pl.reciprocal(below, approx=True)
        values = main[:, part * 256 : part * 256 + 256].astype(F32)
        normal[:, part * 256 : part * 256 + 256] = (values * (count * inverse)).astype(BF16)
    total[...] += jnp.dot(normal[...], table[...], preferred_element_type=F32)

    @pl.when(step == STEPS - 1)
    def _():
        rows = jnp.concatenate(
            [
                jnp.broadcast_to(owner_row[...].astype(F32), (64, SEGS)),
                jnp.broadcast_to(slot_row[...].astype(F32), (64, SEGS)),
            ],
            axis=0,
        )
        columns = rows.T.astype(jnp.int32)
        owner_col = columns[:, 0:1]
        slots = columns[:, 64:65]
        station = jnp.zeros_like(slots)
        for edge in range(1, ST_DEV):
            station += (slots >= edge * HOURS).astype(jnp.int32)
        hour = slots - station * HOURS
        whole = owner_col * ST_DEV + station
        hits = whole == iota((1, DEVICES * ST_DEV), 1)
        widths = jnp.sum(jnp.where(hits, width_row[...].astype(F32), 0.0), axis=1, keepdims=True)
        widths = widths.astype(jnp.int32)
        real = total[:, :NBAND] * (1.0 / math.sqrt(L))
        imag = total[:, NBAND:] * (1.0 / math.sqrt(L))
        amplitude = jnp.sqrt(real * real + imag * imag)
        lane = iota((1, NBAND), 1)
        smooth = amplitude
        for width in range(1, WMAX + 1):
            up = pltpu.roll(amplitude, width, 1)
            down = pltpu.roll(amplitude, NBAND - width, 1)
            both = jnp.where(lane >= width, up, 0.0) + jnp.where(lane < NBAND - width, down, 0.0)
            smooth += jnp.where(widths >= width, both, 0.0)
        number = jnp.minimum(lane + widths, NBAND - 1) - jnp.maximum(lane - widths, 0) + 1
        factor = 1.0 / jnp.maximum(smooth / number.astype(F32), FLOOR)
        lanes = iota((SEGS, 128), 1)
        extra = jnp.where(
            lanes == 0, station, jnp.where(lanes == 1, hour, jnp.where(lanes == 2, 1, 0))
        )
        whitened = jnp.concatenate(
            [
                (real * factor).astype(BF16),
                (imag * factor).astype(BF16),
                extra.astype(F32).astype(BF16),
            ],
            axis=1,
        )
        same = (owner_col == owner_row[...]) & (iota((SEGS, SEGS), 0) < iota((SEGS, SEGS), 1))
        ones = jnp.ones((8, SEGS), BF16)
        rank = jnp.dot(ones, same.astype(F32).astype(BF16), preferred_element_type=F32)
        rank = rank[0:1].astype(jnp.int32)
        target = owner_row[...] * CAP + rank
        for part in range(4):
            chosen = target == iota((512, SEGS), 0) + part * 512
            chosen = jnp.where(chosen, 1.0, 0.0).astype(BF16)
            picked = jnp.dot(chosen, whitened, preferred_element_type=F32)
            tags = picked[:, 2 * NBAND :].reshape(32, CAP, 128)
            tags = tags[:, :8] + pltpu.roll(tags[:, 8:], 64, 2)
            send[part * 32 : part * 32 + 32, 4 * CAP :, :] = tags.astype(BF16)
            picked = picked.astype(BF16)
            for tile in range(4):
                send[part * 32 : part * 32 + 32, tile * CAP : tile * CAP + CAP, :] = picked[
                    :, tile * 128 : tile * 128 + 128
                ].reshape(32, CAP, 128)


def transform(traces, seg_owner, seg_slot, white_width, band_bins):
    return pl.pallas_call(
        transform_kernel,
        grid=(STEPS,),
        in_specs=[
            pl.BlockSpec((SEGS, STEP), lambda k: (0, k)),
            pl.BlockSpec((SEGS, 128), lambda k: (0, jnp.maximum(k * (STEP // 128) - 1, 0))),
            pl.BlockSpec(
                (SEGS, 128), lambda k: (0, jnp.minimum((k + 1) * (STEP // 128), L // 128 - 1))
            ),
            pl.BlockSpec((1, SEGS), lambda k: (0, 0)),
            pl.BlockSpec((1, SEGS), lambda k: (0, 0)),
            pl.BlockSpec((1, DEVICES * ST_DEV), lambda k: (0, 0)),
            pl.BlockSpec((1, NBAND), lambda k: (0, 0)),
        ],
        out_specs=pl.BlockSpec((DEVICES, TAGGED, 128), lambda k: (0, 0, 0)),
        out_shape=jax.ShapeDtypeStruct((DEVICES, TAGGED, 128), BF16),
        scratch_shapes=[
            pltpu.VMEM((128, NBAND), F32),
            pltpu.VMEM((128, NBAND), F32),
            pltpu.VMEM((64, NBAND), F32),
            pltpu.VMEM((64, NBAND), F32),
            pltpu.VMEM((512, 256), BF16),
            pltpu.VMEM((SEGS, STEP + 256), BF16),
            pltpu.VMEM((SEGS, STEP), BF16),
            pltpu.VMEM((STEP, 2 * NBAND), BF16),
            pltpu.VMEM((SEGS, 2 * NBAND), F32),
        ],
        compiler_params=pltpu.CompilerParams(vmem_limit_bytes=58 << 20),
        cost_estimate=pl.CostEstimate(
            flops=10 * SEGS * L * 512, bytes_accessed=SEGS * L * 2, transcendentals=SEGS * L
        ),
        name="transform",
    )(
        traces, traces, traces, seg_owner.reshape(1, SEGS), seg_slot.reshape(1, SEGS),
        white_width.reshape(1, -1), band_bins.reshape(1, -1),
    )


def stack_kernel(received, spectra, wide):
    tags = received[:, 4 * CAP :, :].astype(F32)
    tags = jnp.concatenate([tags, pltpu.roll(tags, 64, 2)], axis=1).reshape(DEVICES * CAP, 128)
    column = (tags[:, 0:1] * 128.0 + tags[:, 1:2] + (tags[:, 2:3] - 1.0)).astype(jnp.int32)
    total = None
    block = 512
    for part in range(DEVICES * CAP // block):
        sources = slice(part * block // CAP, (part + 1) * block // CAP)
        hits = column[part * block : (part + 1) * block] == iota((1, ST_DEV * 128), 1)
        hits = jnp.where(hits, 1.0, 0.0).astype(BF16)
        values = jnp.concatenate(
            [
                received[sources, tile * CAP : tile * CAP + CAP, :].reshape(block, 128)
                for tile in range(4)
            ],
            axis=1,
        )
        term = lax.dot_general(values, hits, (((0,), (0,)), ((), ())), preferred_element_type=F32)
        total = term if total is None else total + term
    lane = iota((PAIRS, 128), 1)
    for half in range(2):
        rows = half * 128
        for station in range(ST_DEV):
            lanes = slice(station * 128, station * 128 + 128)
            real_first = total[rows : rows + 64, lanes]
            real_second = pltpu.roll(total[rows + 64 : rows + 128, lanes], 64, 1)
            imag_first = pltpu.roll(total[rows + 256 : rows + 320, lanes], 96, 1)
            imag_second = pltpu.roll(total[rows + 320 : rows + 384, lanes], 32, 1)
            wide[:, station, 0:128] = jnp.where(lane < 96, real_first, imag_first)
            wide[:, station, 128:256] = jnp.where(lane < 64, imag_first, real_second)
            wide[:, station, 256:384] = jnp.where(lane < 32, real_second, imag_second)
        spectra[half * PAIRS * ST_DEV : (half + 1) * PAIRS * ST_DEV] = (
            wide[...].reshape(PAIRS * ST_DEV, WIDE).astype(BF16)
        )


def stack(received):
    return pl.pallas_call(
        stack_kernel,
        out_shape=jax.ShapeDtypeStruct((2 * PAIRS * ST_DEV, WIDE), BF16),
        scratch_shapes=[pltpu.VMEM((PAIRS, ST_DEV, WIDE), F32)],
        compiler_params=pltpu.CompilerParams(vmem_limit_bytes=40 << 20),
        cost_estimate=pl.CostEstimate(
            flops=2 * 2048 * 1024 * 256 * 2, bytes_accessed=3 << 20, transcendentals=0
        ),
        name="stack",
    )(received)


BLOCK = 32
BLOCKS = PAIRS // BLOCK
OUT_ROWS = 16
STRIDE = 2 * 2 * PAIRS + 8


def cross_kernel(places, *refs):
    rows, columns = refs[0:8], list(refs[8:16])
    early, late, beside_left, beside_far = refs[16:20]
    out, row_blocks, column_blocks, left, right, swapped, swap, results, arrived = refs[20:]
    columns += [early.at[0], early.at[1], early.at[2], beside_left]
    columns += [early.at[3], late.at[1], late.at[0], beside_far]
    step = pl.program_id(0)

    def copies(block):
        size = BLOCK * ST_DEV
        at = pl.ds(pl.multiple_of(block * size, size), size)
        out = []
        for index in range(24):
            if index < 8:
                source, target = rows[index], row_blocks
            else:
                source, target = columns[index - 8], column_blocks
            out.append(
                pltpu.make_async_copy(
                    source.at[at], target.at[places[index], at], arrived.at[block, index]
                )
            )
        return out

    @pl.when(step == 0)
    def _():
        @pl.loop(0, 2 * BLOCKS)
        def _(block):
            for copy in copies(block):
                copy.start()

        for part in range(2):
            source = iota((256, 256), 0) + part * 128
            target = iota((256, 256), 1) + part * 128
            mine = target // (2 * HOURS) == part
            group = (target // HOURS) % 2
            ahead = mine & (source == target + HOURS) & (group == 0)
            behind = mine & (source == target - HOURS) & (group == 1)
            swap[part] = (jnp.where(ahead, 1.0, 0.0) - jnp.where(behind, 1.0, 0.0)).astype(BF16)

    @pl.when(step < 2 * BLOCKS)
    def _():
        for copy in copies(step):
            copy.wait()

    @pl.when(step < 2 * BLOCKS)
    def _():
        size = BLOCK * ST_DEV
        whole = pl.ds(pl.multiple_of(step * size, size), size)
        for blocks, target, count in ((row_blocks, left, 8), (column_blocks, right, 16)):
            for index in range(0, count, 2):
                both = [
                    blocks[index + k, whole, :].astype(F32).reshape(BLOCK, ST_DEV, WIDE)
                    for k in range(2)
                ]
                target[:, index * ST_DEV : (index + 2) * ST_DEV, :] = jnp.concatenate(
                    both, axis=1
                ).astype(BF16)
        plain = left[...].reshape(BLOCK * 64, WIDE)
        for part in range(2):
            lanes = slice(part * 128, part * 128 + 256)
            swapped[part] = (
                jnp.dot(plain[:, lanes], swap[part], preferred_element_type=F32)
                .astype(BF16)
                .reshape(BLOCK, 64, 256)
            )
        lane = iota((1, 256), 1)
        first_mask = jnp.where(lane < 2 * HOURS, 1.0, 0.0).astype(BF16)
        second_mask = jnp.where(lane >= 2 * HOURS - 128, 1.0, 0.0).astype(BF16)

        @pl.loop(0, BLOCK, unroll=32)
        def _(pair):
            for part, mask in ((0, first_mask), (1, second_mask)):
                lanes = slice(part * 128, part * 128 + 256)
                rows = jnp.concatenate([left[pair, :, lanes] * mask, swapped[part, pair]], axis=0)
                product = lax.dot_general(
                    rows,
                    right[pair, :, lanes],
                    (((1,), (1,)), ((), ())),
                    preferred_element_type=F32,
                )
                at = step * BLOCK + (step // BLOCKS) * PAIRS + pair + part * PAIRS
                results[pl.ds(at, 128, stride=STRIDE), :] = product

    @pl.when(step >= 2 * BLOCKS)
    def _():
        first = (step - 2 * BLOCKS) * OUT_ROWS
        for row in range(OUT_ROWS):
            for part in range(2):
                for half in range(2):
                    at = (first + row + part * 64) * STRIDE + half * 128
                    lanes = slice(part * NBAND + half * 128, part * NBAND + half * 128 + 128)
                    product = results[pl.ds(pl.multiple_of(at, 8), 128), :]
                    out[row, :, lanes] = product.T.astype(BF16)


def cross(places, rows, columns):
    return pl.pallas_call(
        cross_kernel,
        grid=(2 * BLOCKS + 64 // OUT_ROWS,),
        in_specs=[pl.BlockSpec(memory_space=pltpu.SMEM)] + [pl.BlockSpec(memory_space=pltpu.HBM)] * 20,
        out_specs=pl.BlockSpec(
            (OUT_ROWS, 128, 2 * NBAND), lambda step: (jnp.maximum(step - 2 * BLOCKS, 0), 0, 0)
        ),
        out_shape=jax.ShapeDtypeStruct((64, 128, 2 * NBAND), BF16),
        scratch_shapes=[
            pltpu.VMEM((8, 2 * PAIRS * ST_DEV, WIDE), BF16),
            pltpu.VMEM((16, 2 * PAIRS * ST_DEV, WIDE), BF16),
            pltpu.VMEM((BLOCK, 64, WIDE), BF16),
            pltpu.VMEM((BLOCK, 128, WIDE), BF16),
            pltpu.VMEM((2, BLOCK, 64, 256), BF16),
            pltpu.VMEM((2, 256, 256), BF16),
            pltpu.VMEM((129 * STRIDE, 128), F32),
            pltpu.SemaphoreType.DMA((2 * BLOCKS, 24)),
        ],
        compiler_params=pltpu.CompilerParams(vmem_limit_bytes=58 << 20),
        cost_estimate=pl.CostEstimate(
            flops=2 * 128 * 128 * 256 * 128 * 3, bytes_accessed=14 << 20, transcendentals=0
        ),
        name="cross",
    )(places, *rows, *columns)


def ring(size, shift):
    return [(i, (i + shift) % size) for i in range(size)]


def move(array, axis, pairs, *others):
    return lax.ppermute(lax.optimization_barrier((array,) + others)[0], axis, pairs)


UP, DOWN, SWAP = ring(4, 1), ring(4, 3), [(0, 1), (1, 0)]


def gather(own):
    q = move(own, "zh", SWAP)
    lx, rx = move(own, "x", UP), move(own, "x", DOWN)
    ly, ry = move(own, "y", UP), move(own, "y", DOWN)
    p = move(own, "zl", SWAP, ly, ry)
    fx = move(lx, "x", UP, rx)
    fy, rq = move(ly, "y", UP, ry), move(q, "y", DOWN, ry)
    s_early = move(jnp.stack([own, q, ly, ry]), "core", SWAP, lx, rx)
    lp, rp = move(p, "x", UP, fx), move(p, "x", DOWN, fx)
    lq, gq = move(q, "y", UP, fy, rq), move(rq, "y", DOWN, fy)
    gp = move(fx, "zl", SWAP, p, s_early)
    s_late = move(jnp.stack([fy, rq]), "core", SWAP, s_early, lp, rp)
    s_lq = move(lq, "core", SWAP, gp)
    s_gq = move(gq, "core", SWAP, gp)
    rows = [own, p, lx, lp, rx, rp, fx, gp]
    columns = [own, q, ly, lq, ry, rq, fy, gq, s_early, s_late, s_lq, s_gq]
    return rows, columns


def block_places():
    zh, y, core, x, zl = (lax.axis_index(name) for name in AXES)
    out = []
    for shift in (0, 3, 1, 2):
        there = (x + shift) % 4
        out += [there * 2 + zl, there * 2 + (1 - zl)]
    for own in (core, 1 - core):
        for shift in (0, 3, 1, 2):
            there = (y + shift) % 4
            out += [zh * 8 + there * 2 + own, (1 - zh) * 8 + there * 2 + own]
    return jnp.stack(out).astype(jnp.int32)


def on_device(traces, seg_owner, seg_slot, white_width, band_bins):
    send = transform(traces, seg_owner, seg_slot, white_width, band_bins)
    places = block_places()
    received = lax.all_to_all(send, AXES, split_axis=0, concat_axis=0, tiled=True)
    own = stack(received)
    rows, columns = gather(own)
    return cross(places, rows, columns)


def solution(mesh):
    fine = Mesh(mesh.devices.reshape(2, 4, 2, 4, 2), AXES)
    return jax.shard_map(
        on_device,
        mesh=fine,
        in_specs=(P(AXES, None), P(AXES, None), P(AXES), P(), P()),
        out_specs=P(("zh", "y", "core"), ("x", "zl"), None),
        check_vma=False,
    )
```

```python
import math

import jax
import jax.numpy as jnp
from jax import lax
from jax.experimental import pallas as pl
from jax.experimental.pallas import tpu as pltpu
from jax.sharding import Mesh, PartitionSpec as P

L = 8192
NBAND = 256
HALF = 64
WMAX = 8
ST_DEV = 8
HOURS = 96
CAP = 16
EPS = 1e-05
FLOOR = 0.5

AXES = ("zh", "y", "core", "x", "zl")
DEVICES = 128
SEGS = 512
STEP = 2048
STEPS = L // STEP
PAIRS = 64
WIDE = 4 * HOURS
TAGGED = 4 * CAP + 8
F32 = jnp.float32
BF16 = jnp.bfloat16


def iota(shape, axis):
    return lax.broadcasted_iota(jnp.int32, shape, axis)


def transform_kernel(
    main, before, after, owner_row, slot_row, width_row, bins,
    send, low_cos, low_sin, high_cos, high_sin, band, magnitude, normal, table, total,
):
    step = pl.program_id(0)

    @pl.when(step == 0)
    def _():
        unit = 2.0 * math.pi / L
        phase = (iota((128, NBAND), 0) * bins[...]) & (L - 1)
        angle = phase.astype(F32) * unit
        low_cos[...] = jnp.cos(angle)
        low_sin[...] = jnp.sin(angle)
        phase = (iota((64, NBAND), 0) * 128 * bins[...]) & (L - 1)
        angle = phase.astype(F32) * unit
        high_cos[...] = jnp.cos(angle)
        high_sin[...] = jnp.sin(angle)
        offset = iota((512, 256), 0) - 128 - iota((512, 256), 1)
        band[...] = jnp.where(jnp.abs(offset) <= HALF, 1.0, 0.0).astype(BF16)
        total[...] = jnp.zeros_like(total)

    for part in range(STEP // 128):
        high = step * (STEP // 128) + part
        cos_high = high_cos[pl.ds(high, 1), :]
        sin_high = high_sin[pl.ds(high, 1), :]
        rows = slice(part * 128, part * 128 + 128)
        table[rows, :NBAND] = (cos_high * low_cos[...] - sin_high * low_sin[...]).astype(BF16)
        table[rows, NBAND:] = (-(sin_high * low_cos[...] + cos_high * low_sin[...])).astype(BF16)

    magnitude[:, 128 : 128 + STEP] = jnp.abs(main[...])
    magnitude[:, :128] = jnp.where(step > 0, jnp.abs(before[...]), jnp.zeros((), BF16))
    magnitude[:, 128 + STEP :] = jnp.where(
        step < STEPS - 1, jnp.abs(after[...]), jnp.zeros((), BF16)
    )
    for part in range(STEP // 256):
        sums = jnp.dot(
            magnitude[:, part * 256 : part * 256 + 512], band[...], preferred_element_type=F32
        )
        place = step * STEP + part * 256 + iota((1, 256), 1)
        count = jnp.minimum(place + HALF, L - 1) - jnp.maximum(place - HALF, 0) + 1
        count = count.astype(F32)
        below = sums + count * EPS
        inverse = pl.reciprocal(below, approx=True)
        values = main[:, part * 256 : part * 256 + 256].astype(F32)
        normal[:, part * 256 : part * 256 + 256] = (values * (count * inverse)).astype(BF16)
    total[...] += jnp.dot(normal[...], table[...], preferred_element_type=F32)

    @pl.when(step == STEPS - 1)
    def _():
        rows = jnp.concatenate(
            [
                jnp.broadcast_to(owner_row[...].astype(F32), (64, SEGS)),
                jnp.broadcast_to(slot_row[...].astype(F32), (64, SEGS)),
            ],
            axis=0,
        )
        columns = rows.T.astype(jnp.int32)
        owner_col = columns[:, 0:1]
        slots = columns[:, 64:65]
        station = jnp.zeros_like(slots)
        for edge in range(1, ST_DEV):
            station += (slots >= edge * HOURS).astype(jnp.int32)
        hour = slots - station * HOURS
        whole = owner_col * ST_DEV + station
        hits = whole == iota((1, DEVICES * ST_DEV), 1)
        widths = jnp.sum(jnp.where(hits, width_row[...].astype(F32), 0.0), axis=1, keepdims=True)
        widths = widths.astype(jnp.int32)
        real = total[:, :NBAND] * (1.0 / math.sqrt(L))
        imag = total[:, NBAND:] * (1.0 / math.sqrt(L))
        amplitude = jnp.sqrt(real * real + imag * imag)
        lane = iota((1, NBAND), 1)
        padded = jnp.concatenate([amplitude, jnp.zeros((SEGS, 128), F32)], axis=1)
        smooth = amplitude
        for width in range(1, WMAX + 1):
            up = pltpu.roll(padded, width, 1)[:, :NBAND]
            down = pltpu.roll(padded, NBAND + 128 - width, 1)[:, :NBAND]
            smooth += jnp.where(widths >= width, up + down, 0.0)
        number = jnp.minimum(lane + widths, NBAND - 1) - jnp.maximum(lane - widths, 0) + 1
        factor = 1.0 / jnp.maximum(smooth / number.astype(F32), FLOOR)
        lanes = iota((SEGS, 128), 1)
        extra = jnp.where(
            lanes == 0, station, jnp.where(lanes == 1, hour, jnp.where(lanes == 2, 1, 0))
        )
        whitened = jnp.concatenate(
            [
                (real * factor).astype(BF16),
                (imag * factor).astype(BF16),
                extra.astype(F32).astype(BF16),
            ],
            axis=1,
        )
        same = (owner_col == owner_row[...]) & (iota((SEGS, SEGS), 0) < iota((SEGS, SEGS), 1))
        ones = jnp.ones((8, SEGS), BF16)
        rank = jnp.dot(ones, same.astype(F32).astype(BF16), preferred_element_type=F32)
        rank = rank[0:1].astype(jnp.int32)
        target = owner_row[...] * CAP + rank
        for part in range(4):
            chosen = target == iota((512, SEGS), 0) + part * 512
            chosen = jnp.where(chosen, 1.0, 0.0).astype(BF16)
            picked = jnp.dot(chosen, whitened, preferred_element_type=F32)
            tags = picked[:, 2 * NBAND :].reshape(32, CAP, 128)
            tags = tags[:, :8] + pltpu.roll(tags[:, 8:], 64, 2)
            send[part * 32 : part * 32 + 32, 4 * CAP :, :] = tags.astype(BF16)
            picked = picked.astype(BF16)
            for tile in range(4):
                send[part * 32 : part * 32 + 32, tile * CAP : tile * CAP + CAP, :] = picked[
                    :, tile * 128 : tile * 128 + 128
                ].reshape(32, CAP, 128)


def transform(traces, seg_owner, seg_slot, white_width, band_bins):
    return pl.pallas_call(
        transform_kernel,
        grid=(STEPS,),
        in_specs=[
            pl.BlockSpec((SEGS, STEP), lambda k: (0, k)),
            pl.BlockSpec((SEGS, 128), lambda k: (0, jnp.maximum(k * (STEP // 128) - 1, 0))),
            pl.BlockSpec(
                (SEGS, 128), lambda k: (0, jnp.minimum((k + 1) * (STEP // 128), L // 128 - 1))
            ),
            pl.BlockSpec((1, SEGS), lambda k: (0, 0)),
            pl.BlockSpec((1, SEGS), lambda k: (0, 0)),
            pl.BlockSpec((1, DEVICES * ST_DEV), lambda k: (0, 0)),
            pl.BlockSpec((1, NBAND), lambda k: (0, 0)),
        ],
        out_specs=pl.BlockSpec((DEVICES, TAGGED, 128), lambda k: (0, 0, 0)),
        out_shape=jax.ShapeDtypeStruct((DEVICES, TAGGED, 128), BF16),
        scratch_shapes=[
            pltpu.VMEM((128, NBAND), F32),
            pltpu.VMEM((128, NBAND), F32),
            pltpu.VMEM((64, NBAND), F32),
            pltpu.VMEM((64, NBAND), F32),
            pltpu.VMEM((512, 256), BF16),
            pltpu.VMEM((SEGS, STEP + 256), BF16),
            pltpu.VMEM((SEGS, STEP), BF16),
            pltpu.VMEM((STEP, 2 * NBAND), BF16),
            pltpu.VMEM((SEGS, 2 * NBAND), F32),
        ],
        compiler_params=pltpu.CompilerParams(vmem_limit_bytes=58 << 20),
        cost_estimate=pl.CostEstimate(
            flops=10 * SEGS * L * 512, bytes_accessed=SEGS * L * 2, transcendentals=SEGS * L
        ),
        name="transform",
    )(
        traces, traces, traces, seg_owner.reshape(1, SEGS), seg_slot.reshape(1, SEGS),
        white_width.reshape(1, -1), band_bins.reshape(1, -1),
    )


def stack_kernel(received, spectra, wide):
    tags = received[:, 4 * CAP :, :].astype(F32)
    tags = jnp.concatenate([tags, pltpu.roll(tags, 64, 2)], axis=1).reshape(DEVICES * CAP, 128)
    column = (tags[:, 0:1] * 128.0 + tags[:, 1:2] + (tags[:, 2:3] - 1.0)).astype(jnp.int32)
    total = None
    block = 512
    for part in range(DEVICES * CAP // block):
        sources = slice(part * block // CAP, (part + 1) * block // CAP)
        hits = column[part * block : (part + 1) * block] == iota((1, ST_DEV * 128), 1)
        hits = jnp.where(hits, 1.0, 0.0).astype(BF16)
        values = jnp.concatenate(
            [
                received[sources, tile * CAP : tile * CAP + CAP, :].reshape(block, 128)
                for tile in range(4)
            ],
            axis=1,
        )
        term = lax.dot_general(values, hits, (((0,), (0,)), ((), ())), preferred_element_type=F32)
        total = term if total is None else total + term
    lane = iota((PAIRS, 128), 1)
    for half in range(2):
        rows = half * 128
        for station in range(ST_DEV):
            lanes = slice(station * 128, station * 128 + 128)
            real_first = total[rows : rows + 64, lanes]
            real_second = pltpu.roll(total[rows + 64 : rows + 128, lanes], 64, 1)
            imag_first = pltpu.roll(total[rows + 256 : rows + 320, lanes], 96, 1)
            imag_second = pltpu.roll(total[rows + 320 : rows + 384, lanes], 32, 1)
            wide[:, station, 0:128] = jnp.where(lane < 96, real_first, imag_first)
            wide[:, station, 128:256] = jnp.where(lane < 64, imag_first, real_second)
            wide[:, station, 256:384] = jnp.where(lane < 32, real_second, imag_second)
        spectra[half * PAIRS * ST_DEV : (half + 1) * PAIRS * ST_DEV] = (
            wide[...].reshape(PAIRS * ST_DEV, WIDE).astype(BF16)
        )


def stack(received):
    return pl.pallas_call(
        stack_kernel,
        out_shape=jax.ShapeDtypeStruct((2 * PAIRS * ST_DEV, WIDE), BF16),
        scratch_shapes=[pltpu.VMEM((PAIRS, ST_DEV, WIDE), F32)],
        compiler_params=pltpu.CompilerParams(vmem_limit_bytes=40 << 20),
        cost_estimate=pl.CostEstimate(
            flops=2 * 2048 * 1024 * 256 * 2, bytes_accessed=3 << 20, transcendentals=0
        ),
        name="stack",
    )(received)


BLOCK = 32
BLOCKS = PAIRS // BLOCK
OUT_ROWS = 16
STRIDE = 2 * 2 * PAIRS + 8


def cross_kernel(places, *refs):
    rows, columns = refs[0:8], list(refs[8:16])
    early, late, beside_left, beside_far = refs[16:20]
    out, row_blocks, column_blocks, left, right, swapped, swap, results, arrived = refs[20:]
    columns += [early.at[0], early.at[1], early.at[2], beside_left]
    columns += [early.at[3], late.at[1], late.at[0], beside_far]
    step = pl.program_id(0)

    def copies(block):
        size = BLOCK * ST_DEV
        at = pl.ds(pl.multiple_of(block * size, size), size)
        out = []
        for index in range(24):
            if index < 8:
                source, target = rows[index], row_blocks
            else:
                source, target = columns[index - 8], column_blocks
            out.append(
                pltpu.make_async_copy(
                    source.at[at], target.at[places[index], at], arrived.at[block, index]
                )
            )
        return out

    @pl.when(step == 0)
    def _():
        @pl.loop(0, 2 * BLOCKS)
        def _(block):
            for copy in copies(block):
                copy.start()

        for part in range(2):
            source = iota((256, 256), 0) + part * 128
            target = iota((256, 256), 1) + part * 128
            mine = target // (2 * HOURS) == part
            group = (target // HOURS) % 2
            ahead = mine & (source == target + HOURS) & (group == 0)
            behind = mine & (source == target - HOURS) & (group == 1)
            swap[part] = (jnp.where(ahead, 1.0, 0.0) - jnp.where(behind, 1.0, 0.0)).astype(BF16)

    @pl.when(step < 2 * BLOCKS)
    def _():
        for copy in copies(step):
            copy.wait()

    @pl.when(step < 2 * BLOCKS)
    def _():
        size = BLOCK * ST_DEV
        whole = pl.ds(pl.multiple_of(step * size, size), size)
        for blocks, target, count in ((row_blocks, left, 8), (column_blocks, right, 16)):
            for index in range(0, count, 2):
                both = [
                    blocks[index + k, whole, :].astype(F32).reshape(BLOCK, ST_DEV, WIDE)
                    for k in range(2)
                ]
                target[:, index * ST_DEV : (index + 2) * ST_DEV, :] = jnp.concatenate(
                    both, axis=1
                ).astype(BF16)
        plain = left[...].reshape(BLOCK * 64, WIDE)
        for part in range(2):
            lanes = slice(part * 128, part * 128 + 256)
            swapped[part] = (
                jnp.dot(plain[:, lanes], swap[part], preferred_element_type=F32)
                .astype(BF16)
                .reshape(BLOCK, 64, 256)
            )
        lane = iota((1, 256), 1)
        first_mask = jnp.where(lane < 2 * HOURS, 1.0, 0.0).astype(BF16)
        second_mask = jnp.where(lane >= 2 * HOURS - 128, 1.0, 0.0).astype(BF16)

        @pl.loop(0, BLOCK, unroll=32)
        def _(pair):
            for part, mask in ((0, first_mask), (1, second_mask)):
                lanes = slice(part * 128, part * 128 + 256)
                rows = jnp.concatenate([left[pair, :, lanes] * mask, swapped[part, pair]], axis=0)
                product = lax.dot_general(
                    rows,
                    right[pair, :, lanes],
                    (((1,), (1,)), ((), ())),
                    preferred_element_type=F32,
                )
                at = step * BLOCK + (step // BLOCKS) * PAIRS + pair + part * PAIRS
                results[pl.ds(at, 128, stride=STRIDE), :] = product

    @pl.when(step >= 2 * BLOCKS)
    def _():
        first = (step - 2 * BLOCKS) * OUT_ROWS
        for row in range(OUT_ROWS):
            for part in range(2):
                for half in range(2):
                    at = (first + row + part * 64) * STRIDE + half * 128
                    lanes = slice(part * NBAND + half * 128, part * NBAND + half * 128 + 128)
                    product = results[pl.ds(pl.multiple_of(at, 8), 128), :]
                    out[row, :, lanes] = product.T.astype(BF16)


def cross(places, rows, columns):
    return pl.pallas_call(
        cross_kernel,
        grid=(2 * BLOCKS + 64 // OUT_ROWS,),
        in_specs=[pl.BlockSpec(memory_space=pltpu.SMEM)] + [pl.BlockSpec(memory_space=pltpu.HBM)] * 20,
        out_specs=pl.BlockSpec(
            (OUT_ROWS, 128, 2 * NBAND), lambda step: (jnp.maximum(step - 2 * BLOCKS, 0), 0, 0)
        ),
        out_shape=jax.ShapeDtypeStruct((64, 128, 2 * NBAND), BF16),
        scratch_shapes=[
            pltpu.VMEM((8, 2 * PAIRS * ST_DEV, WIDE), BF16),
            pltpu.VMEM((16, 2 * PAIRS * ST_DEV, WIDE), BF16),
            pltpu.VMEM((BLOCK, 64, WIDE), BF16),
            pltpu.VMEM((BLOCK, 128, WIDE), BF16),
            pltpu.VMEM((2, BLOCK, 64, 256), BF16),
            pltpu.VMEM((2, 256, 256), BF16),
            pltpu.VMEM((129 * STRIDE, 128), F32),
            pltpu.SemaphoreType.DMA((2 * BLOCKS, 24)),
        ],
        compiler_params=pltpu.CompilerParams(vmem_limit_bytes=58 << 20),
        cost_estimate=pl.CostEstimate(
            flops=2 * 128 * 128 * 256 * 128 * 3, bytes_accessed=14 << 20, transcendentals=0
        ),
        name="cross",
    )(places, *rows, *columns)


def ring(size, shift):
    return [(i, (i + shift) % size) for i in range(size)]


def move(array, axis, pairs, *others):
    return lax.ppermute(lax.optimization_barrier((array,) + others)[0], axis, pairs)


UP, DOWN, SWAP = ring(4, 1), ring(4, 3), [(0, 1), (1, 0)]


def gather(own):
    q = move(own, "zh", SWAP)
    lx, rx = move(own, "x", UP), move(own, "x", DOWN)
    ly, ry = move(own, "y", UP), move(own, "y", DOWN)
    p = move(own, "zl", SWAP, ly, ry)
    fx = move(lx, "x", UP, rx)
    fy, rq = move(ly, "y", UP, ry), move(q, "y", DOWN, ry)
    s_early = move(jnp.stack([own, q, ly, ry]), "core", SWAP, lx, rx)
    lp, rp = move(p, "x", UP, fx), move(p, "x", DOWN, fx)
    lq, gq = move(q, "y", UP, fy, rq), move(rq, "y", DOWN, fy)
    gp = move(fx, "zl", SWAP, p, s_early)
    s_late = move(jnp.stack([fy, rq]), "core", SWAP, s_early, lp, rp)
    s_lq = move(lq, "core", SWAP, gp)
    s_gq = move(gq, "core", SWAP, gp)
    rows = [own, p, lx, lp, rx, rp, fx, gp]
    columns = [own, q, ly, lq, ry, rq, fy, gq, s_early, s_late, s_lq, s_gq]
    return rows, columns


def block_places():
    zh, y, core, x, zl = (lax.axis_index(name) for name in AXES)
    out = []
    for shift in (0, 3, 1, 2):
        there = (x + shift) % 4
        out += [there * 2 + zl, there * 2 + (1 - zl)]
    for own in (core, 1 - core):
        for shift in (0, 3, 1, 2):
            there = (y + shift) % 4
            out += [zh * 8 + there * 2 + own, (1 - zh) * 8 + there * 2 + own]
    return jnp.stack(out).astype(jnp.int32)


def on_device(traces, seg_owner, seg_slot, white_width, band_bins):
    send = transform(traces, seg_owner, seg_slot, white_width, band_bins)
    places = block_places()
    received = lax.all_to_all(send, AXES, split_axis=0, concat_axis=0, tiled=True)
    own = stack(received)
    rows, columns = gather(own)
    return cross(places, rows, columns)


def solution(mesh):
    fine = Mesh(mesh.devices.reshape(2, 4, 2, 4, 2), AXES)
    return jax.shard_map(
        on_device,
        mesh=fine,
        in_specs=(P(AXES, None), P(AXES, None), P(AXES), P(), P()),
        out_specs=P(("zh", "y", "core"), ("x", "zl"), None),
        check_vma=False,
    )
```
